32 devices in a mesh: groups: 2 (over x), grid: 16 (over z, y, core).
Axes of the slice: x: 2, y: 2, z: 4, core: 2. Of those that a mesh axis runs over, the one named last changes fastest.
Arguments:
- ensemble: bfloat16 [1024, 128, 128], P(('groups', 'grid')), parts along dimension 0, may hold values from -8 to 8, as said below
- owner_slot: int32 [256], P('groups'), parts along dimension 0, may hold values from 0 to 127, each once
- weights: float32 [256, 64, 64], P(('groups', 'grid')), parts along dimension 0, may hold values from -0.25 to 1.25, as said below
- obs_members: bfloat16 [1024, 64, 128], P(('groups', 'grid')), parts along dimension 0, may hold values from -2 to 2
- departures: bfloat16 [1024, 128], P(('groups', 'grid')), parts along dimension 0, may hold values from -6 to 6
- obs_count: int32 [1024], P(('groups', 'grid')), parts along dimension 0, may hold values from 1 to 128, 40960 in all
- pair_home: int32 [256, 8], P('groups'), parts along dimension 0, may hold values from 0 to 15, all different within a row; in each aligned block of 8 rows (0 to 7, 8 to 15, ...) at most 8 rows name the same one
- pair_index: int32 [256, 8], P('groups'), parts along dimension 0, may hold values from 0 to 31
- localization: float32 [256, 8], P(('groups', 'grid')), parts along dimension 0, may hold values from 0.2 to 1
Outputs:
- analysis: bfloat16 [1024, 128, 128], P(('groups', 'grid')), parts along dimension 0
- mean_weights: float32 [256, 64], P(('groups', 'grid')), parts along dimension 0
The draws below stay inside these ranges and needn't reach their ends.
There are 2 independent parts, one for each index of `groups`. The reference program is written for one: setup_inputs(seed, part) draws one part's arguments, and reference() takes and returns one part's arrays. A program takes and returns all parts, laid end to end along the dimension named above; each array names one. Nothing has to cross between parts.
Inputs may be any that keep to these rules, and one draw needn't show every extreme that they name: The ensemble is a common field plus member perturbations. `weights`: dominant diagonal with full off-diagonal part. `pair_home`: each slot's 8 pairs name different home devices; among the 8 slots of one device no home device is named by more than 8 pairs. `owner_slot`: each slot once.
All inputs are finite; a program needn't handle non-finite values. No bound on the sum of `obs_count` on one device may be relied on, other than what follows from the above.
Results may differ from the reference program's by a relative error of at most 0.0075.
Values may be sent and summed in bfloat16 or wider, within the bound.
A program may use at most 64 MiB of HBM per device.

```python
import math
import jax
import jax.numpy as jnp
import numpy as np
from jax import lax

K = 64
LEV = 8
P_SIZE = 128
NPAIR = 8
BD = 8
CAP = 8
OD = 32
FIELDS = 512
BLOCKS = 128
OBS_BLOCKS = 512
N_GRID = 16


def draw_ensemble(key, part):
    key = jax.random.fold_in(key, 11)
    key_base, key_pert = jax.random.split(key, 2)
    base = jax.random.normal(key_base, (LEV, BLOCKS, P_SIZE), jnp.float32)
    pert = 0.7 * jax.random.normal(key_pert, (K, LEV, BLOCKS, P_SIZE), jnp.float32)
    values = jnp.clip(base[None] + pert, -8.0, 8.0)
    return values.reshape(FIELDS, BLOCKS, P_SIZE).astype(jnp.bfloat16)


def draw_weights(key, part):
    key = jax.random.fold_in(key, 23)
    key_diag, key_off = jax.random.split(key, 2)
    diagonal = jax.random.uniform(key_diag, (BLOCKS, K), jnp.float32, 0.6, 1.0)
    noise = jnp.clip(jax.random.normal(key_off, (BLOCKS, K, K), jnp.float32), -3.0, 3.0)
    off_part = jnp.clip(noise * (0.5 / math.sqrt(K)), -0.25, 0.25)
    row_ids = jax.lax.broadcasted_iota(jnp.int32, (K, K), 0)
    col_ids = jax.lax.broadcasted_iota(jnp.int32, (K, K), 1)
    identity = (row_ids == col_ids).astype(jnp.float32)
    return off_part + diagonal[:, :, None] * identity[None]


def place_ends(drawn, key, least, largest):
    index_at = [jax.random.randint(jax.random.fold_in(key, axis), (), 0, length) for axis, length in enumerate(drawn.shape)]
    widest = drawn.shape.index(max(drawn.shape))
    neighbour = index_at[:widest] + [(index_at[widest] + 1) % drawn.shape[widest]] + index_at[widest + 1:]
    return drawn.at[tuple(index_at)].set(least).at[tuple(neighbour)].set(largest)


def block_levels(own_key, shape, cuts, smallest, largest):
    def one(axis_at, blocks):
        draws = jax.random.uniform(jax.random.fold_in(jax.random.fold_in(own_key, 6), axis_at), (blocks,), jnp.float32, smallest / len(cuts), largest / len(cuts))
        return jnp.repeat(jnp.exp(draws), shape[axis_at] // blocks).reshape((-1,) + (1,) * (len(shape) - axis_at - 1))

    loudness = one(*cuts[0])
    for cut in cuts[1:]:
        loudness = loudness * one(*cut)
    return loudness


def profile(number_of, total, bound, slope):
    loads = [(1 << 20) // math.isqrt(rank ** slope) + 1 for rank in range(2, number_of + 1)]
    surplus, given = total - bound - (number_of - 1), [1] * (number_of - 1)
    while surplus > 0:
        movable = [i for i in range(number_of - 1) if given[i] < bound]
        whole, budget = sum([loads[i] for i in movable]), surplus
        for i in movable:
            more = min(bound - given[i], max(1, budget * loads[i] // whole), surplus)
            given[i] = given[i] + more
            surplus = surplus - more
    return np.array([bound] + given)


def ragged(key, amount, total, most, slope):
    if amount == 2:
        one = jax.random.randint(key, (), max(1, total - most), min(most, total - 1) + 1)
        return jnp.stack([one, total - one])
    sizes = jnp.asarray(profile(amount, total, most, slope), jnp.int32)
    twos = (amount - 1) // 2
    source_of, sink = sizes[1:1 + 2 * twos:2], sizes[2:2 + 2 * twos:2]
    margin = jnp.minimum(source_of - 1, most - sink)
    shifted = jax.random.randint(jax.random.fold_in(key, 1), (twos,), 0, 1 << 20) % (margin + 1)
    sizes = sizes.at[1:1 + 2 * twos:2].set(source_of - shifted).at[2:2 + 2 * twos:2].set(sink + shifted)
    return sizes[jax.random.permutation(jax.random.fold_in(key, 2), amount)]


def deal_out(own_key, own, number, rows, count, top, bound, slope):
    sequence = jax.random.permutation(own_key, count)
    crowded, usual = portions_of(count, rows * top, bound, slope, True), portions_of(count, rows * top, bound, slope, False)
    places = jnp.arange(count)

    def named(sizes, offset_by):
        used = int((sizes > 0).sum())
        fixed = max(1, used // 4)
        shifted = fixed + (places - fixed + offset_by * (used - fixed)) % max(1, count - fixed)
        return jnp.zeros((count,), jnp.int32).at[sequence[jnp.where(places < fixed, places, shifted)]].set(jnp.asarray(sizes, jnp.int32))

    sizes = jnp.where(number % 4 == 0, named(crowded, number // 4), named(usual, number - number // 4 - 1))
    mixed = jax.random.permutation(jax.random.fold_in(own, 3), count)
    giver, sink = mixed[0:count // 2 * 2:2], mixed[1:count // 2 * 2:2]
    slack = jnp.minimum(sizes[giver] - 1, bound - sizes[sink]) // 2
    slack = jnp.where((giver == sequence[0]) | (sink == sequence[0]) | (sizes[sink] == 0), 0, jnp.maximum(slack, 0))
    shifted = jax.random.randint(jax.random.fold_in(own, 4), (count // 2,), 0, 1 << 20) % (slack + 1)
    sizes = sizes.at[giver].add(-shifted).at[sink].add(shifted)
    members = jnp.searchsorted(jnp.cumsum(sizes), jnp.arange(rows * top), side="right").astype(jnp.int32)
    grid = members.reshape(top, rows).T
    grid = grid[jax.random.permutation(jax.random.fold_in(own, 1), rows)]
    offset_by = jax.random.randint(jax.random.fold_in(own, 2), (rows, 1), 0, top)
    return jnp.take_along_axis(grid, (jnp.arange(top)[None, :] + offset_by) % top, axis=1)


def portions_of(count, total, limit, slope, full):
    weights = [(1 << 20) // math.isqrt(standing ** slope) + 1 for standing in range(1, count + 1)]
    largest = limit if full else min(limit, max(-(-total // count), total * weights[0] // sum(weights)))
    least = 1 if total - largest >= count - 1 else 0
    counts, surplus = [largest] + [least] * (count - 1), total - largest - least * (count - 1)
    while surplus > 0:
        free = [i for i in range(1, count) if counts[i] < largest] or [i for i in range(1, count) if counts[i] < limit]
        pool, remaining = sum([weights[i] for i in free]), surplus
        for i in free:
            extra = min(limit - counts[i], max(1, remaining * weights[i] // pool), surplus)
            counts[i] = counts[i] + extra
            surplus = surplus - extra
    return np.array(counts)


def bell_draw(own_key, shape, width, most, pieces=(), kind=jnp.bfloat16):
    values = width * jax.random.normal(own_key, shape, jnp.float32)
    if pieces:
        values = values * block_levels(own_key, shape, pieces, -0.22, 0.18)
    return jnp.clip(values, -most, most).astype(kind)


def setup_inputs(seed: int = 0, part: int = 0) -> dict:
    streams_of = jax.random.split(jax.random.key(seed), 10)
    part_keys = jax.random.split(jax.random.fold_in(streams_of[9], part), 10)
    ensemble = draw_ensemble(jax.random.fold_in(jax.random.fold_in(streams_of[9], part), 71), part)
    owner_slot = jax.random.permutation(part_keys[1], BLOCKS).astype(jnp.int32)
    weights = draw_weights(jax.random.fold_in(jax.random.fold_in(streams_of[9], part), 71), part)
    obs_members = bell_draw(part_keys[3], (OBS_BLOCKS, K, P_SIZE), 0.3, 2.0, ((0, 16),))
    departures = bell_draw(part_keys[4], (OBS_BLOCKS, P_SIZE), 1.0, 6.0, ((0, 16),))
    obs_count = ragged(part_keys[5], OBS_BLOCKS, OBS_BLOCKS * P_SIZE * 5 // 8, P_SIZE, 2).astype(jnp.int32)
    pair_home_keys = jax.random.split(jax.random.fold_in(part_keys[6], 1), BLOCKS // BD)
    pair_home_turns = jax.random.permutation(jax.random.fold_in(part_keys[6], 3), BLOCKS // BD)
    pair_home = jax.vmap(lambda own, number: deal_out(jax.random.fold_in(part_keys[6], 2), own, number, BD, N_GRID, NPAIR, CAP, 1))(pair_home_keys, pair_home_turns).reshape((BLOCKS, NPAIR))
    pair_index = place_ends(jax.random.randint(part_keys[7], (BLOCKS, NPAIR), 0, OD), jax.random.fold_in(part_keys[7], 1), 0, OD - 1).astype(jnp.int32)
    localization = jnp.clip(0.2 + 0.8 * jax.random.uniform(part_keys[8], (BLOCKS, NPAIR), jnp.float32) ** block_levels(part_keys[8], (BLOCKS, NPAIR), ((0, 16),), -0.2, 0.2), 0.2, 1.0)
    return {"ensemble": ensemble, "owner_slot": owner_slot, "weights": weights, "obs_members": obs_members, "departures": departures, "obs_count": obs_count, "pair_home": pair_home, "pair_index": pair_index, "localization": localization}


def reference(ensemble, owner_slot, weights, obs_members, departures, obs_count, pair_home, pair_index, localization):
    slot_pos = lax.broadcasted_iota(jnp.int32, departures.shape, 1)
    masked = jnp.where(slot_pos < obs_count[:, None], departures, jnp.zeros_like(departures))
    obs_sums = jnp.einsum("okp,op->ok", obs_members.astype(jnp.float32), masked.astype(jnp.float32))
    obs_block = (pair_home * OD + pair_index).astype(jnp.int32)
    pair_sums = obs_sums[obs_block]
    innovation = jnp.sum(localization[:, :, None] * pair_sums, axis=1)
    projected = jnp.einsum("bmi,bm->bi", weights, innovation, precision=lax.Precision.HIGHEST)
    mean_weights = jnp.einsum("bji,bi->bj", weights, projected, precision=lax.Precision.HIGHEST) / (K - 1)
    transform = (weights + mean_weights[:, :, None]).astype(jnp.bfloat16)
    column_totals = jnp.sum(transform.astype(jnp.float32), axis=1)
    natural_transform = transform[owner_slot]
    natural_totals = column_totals[owner_slot]
    states = ensemble.reshape(K, LEV, BLOCKS, P_SIZE)

    def one_group(group_index):
        first_row = (group_index * BD).astype(jnp.int32)
        members_now = lax.dynamic_slice_in_dim(states, first_row, BD, 2)
        transform_now = lax.dynamic_slice_in_dim(natural_transform, first_row, BD, 0)
        totals_now = lax.dynamic_slice_in_dim(natural_totals, first_row, BD, 0)
        ens_mean = jnp.sum(members_now.astype(jnp.float32), axis=0) / K
        product = jnp.einsum("jlbp,bji->ilbp", members_now.astype(jnp.float32), transform_now.astype(jnp.float32))
        return (product + ens_mean[None] * (1.0 - totals_now).T[:, None, :, None]).astype(jnp.bfloat16)

    groups_out = lax.map(one_group, jnp.arange(N_GRID).astype(jnp.int32))
    analysis = jnp.transpose(groups_out, (1, 2, 0, 3, 4)).reshape(FIELDS, BLOCKS, P_SIZE)
    return analysis, mean_weights
```

```python
import functools

import jax
import jax.numpy as jnp
from jax import lax
from jax.experimental import pallas as pl
from jax.experimental.pallas import tpu as pltpu
from jax.sharding import PartitionSpec as P

LEV = 8
LANES = 128
F32 = jnp.float32
BF16 = jnp.bfloat16
HIGHEST = lax.Precision.HIGHEST


def iota(shape, dim):
    return lax.broadcasted_iota(jnp.int32, shape, dim)


def one_hot(cond):
    return jnp.where(cond, 1.0, 0.0).astype(BF16)


def dot(a, b):
    return jnp.dot(a, b, preferred_element_type=F32)


def dot_nt(a, b, precision=None):
    return lax.dot_general(
        a, b, (((1,), (1,)), ((), ())), preferred_element_type=F32, precision=precision
    )


def peer_order(n):
    return sorted(range(1, n), key=lambda k: -min(k, n - k))


def fused_kernel(
    dims,
    ens_ref,
    owner_ref,
    weights_ref,
    obs_ref,
    dep_ref,
    count_ref,
    home_ref,
    index_ref,
    loc_ref,
    out_ref,
    mw_ref,
    obs_box,
    send_box,
    recv_box,
    ret_box,
    back_box,
    gather_mat,
    scatter_mat,
    mix_mat,
    gain_ref,
    obs_send,
    obs_recv,
    fwd_send,
    fwd_recv,
    bwd_send,
    bwd_recv,
):
    n, groups = dims
    me = lax.axis_index("grid")
    rows_here, blocks, points = ens_ref.shape
    block_dev, members, _ = weights_ref.shape
    obs_dev = obs_ref.shape[0]
    pair_count = home_ref.shape[1]
    held = rows_here // LEV
    slab = held * block_dev
    full = n * slab
    lev_group = LEV // groups
    width = lev_group * points
    packed = obs_dev // 2
    peers = peer_order(n)

    barrier = pltpu.get_barrier_semaphore()

    def greet(k, carry):
        pl.semaphore_signal(
            barrier,
            inc=1,
            device_id={"grid": lax.rem(me + k, n)},
            device_id_type=pl.DeviceIdType.MESH,
        )
        return carry

    lax.fori_loop(1, n, greet, 0)

    lane = iota((obs_dev, points), 1)
    dep = dep_ref[...].astype(F32)
    masked = jnp.where(lane < count_ref[...], dep, 0.0).astype(BF16)
    cross = dot_nt(masked, obs_ref[...].reshape(obs_dev * members, points))
    row = iota((obs_dev, LANES), 0)
    lane_block = iota((obs_dev, LANES), 1) // members
    per_row = LANES // members
    sums = jnp.zeros((obs_dev, LANES), F32)
    for t in range(obs_dev * members // LANES):
        piece = cross[:, t * LANES : (t + 1) * LANES]
        sums = sums + jnp.where(row == lane_block + t * per_row, piece, 0.0)
    fold = one_hot(iota((packed, obs_dev), 0) == iota((packed, obs_dev), 1) // 2)
    obs_box[pl.ds(me, 1)] = dot(fold, sums.astype(BF16)).astype(BF16)[None]

    r = iota((full, 1), 0)
    row_key = (r // block_dev % held) * blocks + (r // slab) * block_dev + r % block_dev
    owner = jnp.concatenate([owner_ref[...]] * held, axis=1)
    col_key = owner + iota((1, full), 1) // blocks * blocks
    gather_mat[...] = one_hot(row_key == col_key)

    def arrange(g):
        cols = []
        for l in range(g * lev_group, (g + 1) * lev_group):
            cols.append(
                jnp.concatenate([ens_ref[m * LEV + l] for m in range(held)], axis=0)
            )
        state = jnp.concatenate(cols, axis=1)
        sorted_state = dot(gather_mat[...], state).astype(BF16)
        send_box[g] = sorted_state.reshape(n, slab, width)
        recv_box[g, pl.ds(me, 1)] = send_box[g, pl.ds(me, 1)]

    def obs_copy(k):
        to = lax.rem(me + k, n)
        return pltpu.make_async_remote_copy(
            src_ref=obs_box.at[me],
            dst_ref=obs_box.at[me],
            send_sem=obs_send.at[k],
            recv_sem=obs_recv.at[me],
            device_id={"grid": to},
            device_id_type=pl.DeviceIdType.MESH,
        )

    def box_copy(src, dst, send_sem, recv_sem, g, k):
        to = lax.rem(me + k, n)
        return pltpu.make_async_remote_copy(
            src_ref=src.at[g, to],
            dst_ref=dst.at[g, me],
            send_sem=send_sem.at[g, k],
            recv_sem=recv_sem.at[g, me],
            device_id={"grid": to},
            device_id_type=pl.DeviceIdType.MESH,
        )

    def box_arrival(dst, send_sem, recv_sem, g, k):
        src = lax.rem(me + k, n)
        return pltpu.make_async_remote_copy(
            src_ref=dst.at[g, src],
            dst_ref=dst.at[g, src],
            send_sem=send_sem.at[g, k],
            recv_sem=recv_sem.at[g, src],
            device_id={"grid": src},
            device_id_type=pl.DeviceIdType.MESH,
        )

    arrange(0)
    pl.semaphore_wait(barrier, n - 1)
    for k in peers:
        obs_copy(k).start()
    for k in peers:
        box_copy(send_box, recv_box, fwd_send, fwd_recv, 0, k).start()
    for g in range(1, groups):
        arrange(g)
        for k in peers:
            box_copy(send_box, recv_box, fwd_send, fwd_recv, g, k).start()

    same = one_hot(iota((full, full), 0) == iota((full, full), 1))
    scatter_mat[...] = dot_nt(same, gather_mat[...]).astype(BF16)

    for k in peers:
        src = lax.rem(me + k, n)
        pltpu.make_async_remote_copy(
            src_ref=obs_box.at[src],
            dst_ref=obs_box.at[src],
            send_sem=obs_send.at[k],
            recv_sem=obs_recv.at[src],
            device_id={"grid": src},
            device_id_type=pl.DeviceIdType.MESH,
        ).wait_recv()
    all_sums = obs_box[...].reshape(n * packed, LANES).astype(F32)
    mine = pl.ds(pl.multiple_of(me * block_dev, block_dev), block_dev)
    home = home_ref[mine, :]
    index = index_ref[mine, :]
    spot = home * packed + index // 2
    odd = index % 2
    loc = loc_ref[...]
    col = iota((block_dev, n * packed), 1)
    pick = [jnp.zeros((block_dev, n * packed), F32) for _ in range(2)]
    for k in range(pair_count):
        hit = col == spot[:, k : k + 1]
        for parity in range(2):
            gate = jnp.where(odd[:, k : k + 1] == parity, loc[:, k : k + 1], 0.0)
            pick[parity] = pick[parity] + jnp.where(hit, gate, 0.0)
    even_part = jnp.dot(pick[0], all_sums, precision=HIGHEST, preferred_element_type=F32)
    odd_part = jnp.dot(pick[1], all_sums, precision=HIGHEST, preferred_element_type=F32)
    innovation = even_part[:, :members] + odd_part[:, members:]

    weights = weights_ref[...]
    flat = weights.reshape(block_dev * members, members)
    twice = jnp.concatenate([innovation, innovation], axis=1)
    spread = jnp.concatenate([twice] * (block_dev // 2), axis=1)
    spread_row = iota((block_dev, block_dev * members), 0)
    spread_col = iota((block_dev, block_dev * members), 1) // members
    spread = jnp.where(spread_row == spread_col, spread, 0.0)
    projected = jnp.dot(spread, flat, precision=HIGHEST, preferred_element_type=F32)
    mean_w = jnp.sum(weights * projected[:, None, :], axis=2, keepdims=True) / (members - 1)
    mw_ref[...] = jnp.sum(weights * projected[:, None, :], axis=2) / (members - 1)
    transform = (weights + mean_w).astype(BF16).reshape(block_dev * members, members)

    rr = iota((full, full), 0)
    cc = iota((full, full), 1)
    turn = one_hot((rr // block_dev == cc % members) & (rr % block_dev == cc // members))
    turned = dot(turn, transform).astype(BF16)
    repeat = one_hot(iota((full, members), 0) // block_dev == iota((full, members), 1))
    dense = dot_nt(repeat, turned)
    mix_mat[...] = jnp.where(rr % block_dev == cc % block_dev, dense, 0.0).astype(BF16)
    totals = dot(mix_mat[...], jnp.ones((full, width), BF16))
    gain_ref[...] = (1.0 - totals) * (1.0 / members)
    sum_mat = one_hot(iota((block_dev, full), 0) == iota((block_dev, full), 1) % block_dev)

    for g in range(groups):
        for k in peers:
            box_arrival(recv_box, fwd_send, fwd_recv, g, n - k).wait_recv()
        state = recv_box[g].reshape(full, width)
        product = dot(mix_mat[...], state).reshape(members, block_dev, width)
        member_sum = dot(sum_mat, state)
        gain = gain_ref[...].reshape(members, block_dev, width)
        analysis = (product + gain * member_sum[None]).astype(BF16)
        ret_box[g] = analysis.reshape(n, slab, width)
        back_box[g, pl.ds(me, 1)] = ret_box[g, pl.ds(me, 1)]
        for k in peers:
            box_copy(ret_box, back_box, bwd_send, bwd_recv, g, k).start()

    for g in range(groups):
        for k in peers:
            box_arrival(back_box, bwd_send, bwd_recv, g, n - k).wait_recv()
        final = dot(scatter_mat[...], back_box[g].reshape(full, width)).astype(BF16)
        for l in range(lev_group):
            for m in range(held):
                out_ref[m * LEV + g * lev_group + l] = final[
                    m * blocks : (m + 1) * blocks, l * points : (l + 1) * points
                ]

    for k in peers:
        obs_copy(k).wait_send()
        for g in range(groups):
            box_copy(send_box, recv_box, fwd_send, fwd_recv, g, k).wait_send()
            box_copy(ret_box, back_box, bwd_send, bwd_recv, g, k).wait_send()


def fused(
    ensemble,
    owner_slot,
    weights,
    obs_members,
    departures,
    obs_count,
    pair_home,
    pair_index,
    localization,
    groups=4,
):
    n = lax.axis_size("grid")
    rows_here, blocks, points = ensemble.shape
    block_dev, members, _ = weights.shape
    held = rows_here // LEV
    slab = held * block_dev
    full = n * slab
    width = LEV // groups * points
    obs_dev = obs_members.shape[0]
    box = pltpu.VMEM((groups, n, slab, width), BF16)
    vmem = pl.BlockSpec(memory_space=pltpu.VMEM)
    return pl.pallas_call(
        functools.partial(fused_kernel, (n, groups)),
        out_shape=(
            jax.ShapeDtypeStruct(ensemble.shape, BF16),
            jax.ShapeDtypeStruct((block_dev, members), F32),
        ),
        in_specs=[vmem] * 9,
        out_specs=(vmem, vmem),
        scratch_shapes=[
            pltpu.VMEM((n, obs_dev // 2, LANES), BF16),
            box,
            box,
            box,
            box,
            pltpu.VMEM((full, full), BF16),
            pltpu.VMEM((full, full), BF16),
            pltpu.VMEM((full, full), BF16),
            pltpu.VMEM((full, width), F32),
            pltpu.SemaphoreType.DMA((n,)),
            pltpu.SemaphoreType.DMA((n,)),
            pltpu.SemaphoreType.DMA((groups, n)),
            pltpu.SemaphoreType.DMA((groups, n)),
            pltpu.SemaphoreType.DMA((groups, n)),
            pltpu.SemaphoreType.DMA((groups, n)),
        ],
        compiler_params=pltpu.CompilerParams(
            collective_id=0, has_side_effects=True, vmem_limit_bytes=40 * 2**20
        ),
    )(
        ensemble,
        owner_slot.reshape(1, blocks),
        weights,
        obs_members,
        departures,
        obs_count.reshape(obs_dev, 1),
        pair_home,
        pair_index,
        localization,
    )


def staged(
    ensemble,
    owner_slot,
    weights,
    obs_members,
    departures,
    obs_count,
    pair_home,
    pair_index,
    localization,
):
    devices = lax.axis_size("grid")
    my_index = lax.axis_index("grid")
    rows_here, blocks_all, points = ensemble.shape
    block_dev = weights.shape[0]
    members = weights.shape[1]
    pair_count = pair_home.shape[1]
    entries = block_dev * pair_count
    capacity = max(2, 2 * entries // devices)
    slot_pos = lax.broadcasted_iota(jnp.int32, departures.shape, 1)
    masked = jnp.where(slot_pos < obs_count[:, None], departures, jnp.zeros_like(departures))
    homes_all = pair_home.reshape(devices, entries)
    index_all = pair_index.reshape(devices, entries)
    matches = homes_all == my_index
    position = jnp.cumsum(matches.astype(jnp.int32), axis=1) - 1
    slot_ids = jnp.arange(capacity, dtype=jnp.int32)
    select = matches[:, None, :] & (position[:, None, :] == slot_ids[None, :, None])
    picked = jnp.sum(jnp.where(select, index_all[:, None, :], 0), axis=2)
    filled = jnp.any(select, axis=2)
    own_sums = jnp.einsum("okp,op->ok", obs_members, masked, preferred_element_type=jnp.float32)
    send_sums = jnp.where(filled[:, :, None], own_sums[picked], jnp.zeros((), jnp.float32))
    received = lax.all_to_all(send_sums, "grid", split_axis=0, concat_axis=0, tiled=True).reshape(
        devices * capacity, members
    )
    first_row = my_index * block_dev
    my_homes = lax.dynamic_slice_in_dim(pair_home, first_row, block_dev, 0).reshape(entries)
    order_row = lax.broadcasted_iota(jnp.int32, (entries, entries), 0)
    order_col = lax.broadcasted_iota(jnp.int32, (entries, entries), 1)
    earlier = (my_homes[:, None] == my_homes[None, :]) & (order_col < order_row)
    my_position = jnp.sum(earlier.astype(jnp.int32), axis=1)
    item_index = my_homes * capacity + my_position
    pair_sums = received[item_index].reshape(block_dev, pair_count, members)
    innovation = jnp.sum(localization[:, :, None] * pair_sums, axis=1)
    projected = jnp.einsum("bmi,bm->bi", weights, innovation, precision=lax.Precision.HIGHEST)
    mean_weights = jnp.einsum("bji,bi->bj", weights, projected, precision=lax.Precision.HIGHEST) / (
        members - 1
    )
    transform = (weights + mean_weights[:, :, None]).astype(jnp.bfloat16)
    column_totals = jnp.sum(transform.astype(jnp.float32), axis=1)
    inverse = (
        jnp.zeros((blocks_all,), jnp.int32)
        .at[owner_slot]
        .set(jnp.arange(blocks_all, dtype=jnp.int32))
    )
    ordered = ensemble[:, inverse, :]
    owned = lax.all_to_all(ordered, "grid", split_axis=1, concat_axis=0, tiled=True)
    states = owned.reshape(members, LEV, block_dev, points)
    ens_mean = jnp.sum(states, axis=0, dtype=jnp.float32) / members
    product = jnp.einsum("jlbp,bji->ilbp", states, transform, preferred_element_type=jnp.float32)
    analysis = (product + ens_mean[None] * (1.0 - column_totals).T[:, None, :, None]).astype(
        jnp.bfloat16
    )
    returned = lax.all_to_all(
        analysis.reshape(members * LEV, block_dev, points),
        "grid",
        split_axis=0,
        concat_axis=1,
        tiled=True,
    )
    result = returned[:, owner_slot, :]
    return (result, mean_weights)


def per_device(ensemble, owner_slot, weights, *rest):
    rows_here = ensemble.shape[0]
    block_dev = weights.shape[0]
    whole_members = rows_here % LEV == 0
    if whole_members and (rows_here // LEV) * block_dev % 16 == 0:
        return fused(ensemble, owner_slot, weights, *rest)
    return staged(ensemble, owner_slot, weights, *rest)


def solution(mesh):
    placed = (
        P(("groups", "grid"), None, None),
        P("groups"),
        P(("groups", "grid"), None, None),
        P(("groups", "grid"), None, None),
        P(("groups", "grid"), None),
        P(("groups", "grid")),
        P("groups", None),
        P("groups", None),
        P(("groups", "grid"), None),
    )
    return jax.shard_map(
        per_device,
        mesh=mesh,
        in_specs=placed,
        out_specs=(P(("groups", "grid"), None, None), P(("groups", "grid"), None)),
        check_vma=False,
    )
```

```python
import functools

import jax
import jax.numpy as jnp
from jax import lax
from jax.experimental import pallas as pl
from jax.experimental.pallas import tpu as pltpu
from jax.sharding import PartitionSpec as P

LEV = 8
LANES = 128
F32 = jnp.float32
BF16 = jnp.bfloat16
HIGHEST = lax.Precision.HIGHEST


def iota(shape, dim):
    return lax.broadcasted_iota(jnp.int32, shape, dim)


def one_hot(cond):
    return jnp.where(cond, 1.0, 0.0).astype(BF16)


def dot(a, b):
    return jnp.dot(a, b, preferred_element_type=F32)


def dot_nt(a, b, precision=None):
    return lax.dot_general(
        a, b, (((1,), (1,)), ((), ())), preferred_element_type=F32, precision=precision
    )


def peer_order(n):
    return list(range(1, n))


def fused_kernel(
    dims,
    ens_hbm,
    owner_hbm,
    weights_hbm,
    obs_hbm,
    dep_hbm,
    count_hbm,
    home_hbm,
    index_hbm,
    loc_hbm,
    out_hbm,
    mw_hbm,
    ens_ref,
    owner_ref,
    weights_ref,
    obs_ref,
    dep_ref,
    count_ref,
    home_ref,
    index_ref,
    loc_ref,
    out_ref,
    mw_ref,
    obs_box,
    send_box,
    recv_box,
    ret_box,
    back_box,
    gather_mat,
    scatter_mat,
    mix_mat,
    gain_ref,
    load_sem,
    ens_sem,
    out_sem,
    obs_send,
    obs_recv,
    fwd_send,
    fwd_recv,
    bwd_send,
    bwd_recv,
):
    n, groups = dims
    me = lax.axis_index("grid")
    rows_here, blocks, points = ens_ref.shape
    block_dev, members, _ = weights_ref.shape
    obs_dev = obs_ref.shape[0]
    pair_count = home_ref.shape[0]
    held = rows_here // LEV
    slab = held * block_dev
    full = n * slab
    lev_group = LEV // groups
    width = lev_group * points
    packed = obs_dev // 2
    peers = peer_order(n)

    barrier = pltpu.get_barrier_semaphore()
    for k in peers:
        pl.semaphore_signal(
            barrier,
            inc=1,
            device_id={"grid": lax.rem(me + k, n)},
            device_id_type=pl.DeviceIdType.MESH,
        )

    def level_rows(g, m):
        return pl.ds(m * LEV + g * lev_group, lev_group)

    def ens_load(g, m):
        rows = level_rows(g, m)
        return pltpu.make_async_copy(ens_hbm.at[rows], ens_ref.at[rows], ens_sem.at[g, m])

    def out_store(g, m):
        rows = level_rows(g, m)
        return pltpu.make_async_copy(out_ref.at[rows], out_hbm.at[rows], out_sem.at[g, m])

    small = (
        (owner_hbm, owner_ref),
        (obs_hbm, obs_ref),
        (dep_hbm, dep_ref),
        (count_hbm, count_ref),
        (home_hbm, home_ref),
        (index_hbm, index_ref),
        (loc_hbm, loc_ref),
        (weights_hbm, weights_ref),
    )
    loads = [
        pltpu.make_async_copy(src, dst, load_sem.at[i]) for i, (src, dst) in enumerate(small)
    ]
    loads[0].start()
    for g in range(groups):
        for m in range(held):
            ens_load(g, m).start()
    for load in loads[1:]:
        load.start()

    r = iota((full, 1), 0)
    row_key = (r // block_dev % held) * blocks + (r // slab) * block_dev + r % block_dev
    loads[0].wait()
    owner = jnp.concatenate([owner_ref[...]] * held, axis=1)
    col_key = owner + iota((1, full), 1) // blocks * blocks
    gather_mat[...] = one_hot(row_key == col_key)

    def arrange(g):
        for m in range(held):
            ens_load(g, m).wait()
        cols = []
        for l in range(g * lev_group, (g + 1) * lev_group):
            cols.append(
                jnp.concatenate([ens_ref[m * LEV + l] for m in range(held)], axis=0)
            )
        state = jnp.concatenate(cols, axis=1)
        sorted_state = dot(gather_mat[...], state).astype(BF16)
        send_box[g] = sorted_state.reshape(n, slab, width)
        recv_box[g, pl.ds(me, 1)] = send_box[g, pl.ds(me, 1)]

    def obs_copy(k):
        to = lax.rem(me + k, n)
        return pltpu.make_async_remote_copy(
            src_ref=obs_box.at[me],
            dst_ref=obs_box.at[me],
            send_sem=obs_send.at[k],
            recv_sem=obs_recv.at[me],
            device_id={"grid": to},
            device_id_type=pl.DeviceIdType.MESH,
        )

    def box_copy(src, dst, send_sem, recv_sem, g, k):
        to = lax.rem(me + k, n)
        return pltpu.make_async_remote_copy(
            src_ref=src.at[g, to],
            dst_ref=dst.at[g, me],
            send_sem=send_sem.at[g, k],
            recv_sem=recv_sem.at[g, me],
            device_id={"grid": to},
            device_id_type=pl.DeviceIdType.MESH,
        )

    def box_arrival(dst, send_sem, recv_sem, g, k):
        src = lax.rem(me + k, n)
        return pltpu.make_async_remote_copy(
            src_ref=dst.at[g, src],
            dst_ref=dst.at[g, src],
            send_sem=send_sem.at[g, k],
            recv_sem=recv_sem.at[g, src],
            device_id={"grid": src},
            device_id_type=pl.DeviceIdType.MESH,
        )

    arrange(0)
    pl.semaphore_wait(barrier, n - 1)
    for k in peers:
        box_copy(send_box, recv_box, fwd_send, fwd_recv, 0, k).start()

    for load in loads[1:]:
        load.wait()
    lane = iota((obs_dev, points), 1)
    dep = dep_ref[...].astype(F32)
    square = iota((obs_dev, obs_dev), 0) == iota((obs_dev, obs_dev), 1)
    count = jnp.sum(jnp.where(square, count_ref[...], 0), axis=1, keepdims=True)
    masked = jnp.where(lane < count, dep, 0.0).astype(BF16)
    cross = dot_nt(masked, obs_ref[...].reshape(obs_dev * members, points))
    row = iota((obs_dev, LANES), 0)
    lane_block = iota((obs_dev, LANES), 1) // members
    per_row = LANES // members
    sums = jnp.zeros((obs_dev, LANES), F32)
    for t in range(obs_dev * members // LANES):
        piece = cross[:, t * LANES : (t + 1) * LANES]
        sums = sums + jnp.where(row == lane_block + t * per_row, piece, 0.0)
    fold = one_hot(iota((packed, obs_dev), 0) == iota((packed, obs_dev), 1) // 2)
    obs_box[pl.ds(me, 1)] = dot(fold, sums.astype(BF16)).astype(BF16)[None]

    for k in peers:
        obs_copy(k).start()
    for g in range(1, groups):
        arrange(g)
        for k in peers:
            box_copy(send_box, recv_box, fwd_send, fwd_recv, g, k).start()

    same = one_hot(iota((full, full), 0) == iota((full, full), 1))
    scatter_mat[...] = dot_nt(same, gather_mat[...]).astype(BF16)

    for k in peers:
        src = lax.rem(me + k, n)
        pltpu.make_async_remote_copy(
            src_ref=obs_box.at[src],
            dst_ref=obs_box.at[src],
            send_sem=obs_send.at[k],
            recv_sem=obs_recv.at[src],
            device_id={"grid": src},
            device_id_type=pl.DeviceIdType.MESH,
        ).wait_recv()
    all_sums = obs_box[...].reshape(n * packed, LANES).astype(F32)
    mine = one_hot(
        iota((block_dev, blocks), 1) == iota((block_dev, blocks), 0) + me * block_dev
    )
    home = dot_nt(mine, home_ref[...].astype(F32).astype(BF16)).astype(jnp.int32)
    index = dot_nt(mine, index_ref[...].astype(F32).astype(BF16)).astype(jnp.int32)
    spot = home * packed + index // 2
    odd = index % 2
    loc = loc_ref[...]
    col = iota((block_dev, n * packed), 1)
    pick = [jnp.zeros((block_dev, n * packed), F32) for _ in range(2)]
    for k in range(pair_count):
        hit = col == spot[:, k : k + 1]
        for parity in range(2):
            gate = jnp.where(odd[:, k : k + 1] == parity, loc[:, k : k + 1], 0.0)
            pick[parity] = pick[parity] + jnp.where(hit, gate, 0.0)
    even_part = jnp.dot(pick[0], all_sums, precision=HIGHEST, preferred_element_type=F32)
    odd_part = jnp.dot(pick[1], all_sums, precision=HIGHEST, preferred_element_type=F32)
    innovation = even_part[:, :members] + odd_part[:, members:]

    weights = weights_ref[...]
    flat = weights.reshape(block_dev * members, members)
    twice = jnp.concatenate([innovation, innovation], axis=1)
    spread = jnp.concatenate([twice] * (block_dev // 2), axis=1)
    spread_row = iota((block_dev, block_dev * members), 0)
    spread_col = iota((block_dev, block_dev * members), 1) // members
    spread = jnp.where(spread_row == spread_col, spread, 0.0)
    projected = jnp.dot(spread, flat, precision=HIGHEST, preferred_element_type=F32)
    mean_w = jnp.sum(weights * projected[:, None, :], axis=2, keepdims=True) / (members - 1)
    mw_ref[...] = jnp.sum(weights * projected[:, None, :], axis=2) / (members - 1)
    mw_store = pltpu.make_async_copy(mw_ref, mw_hbm, load_sem.at[len(loads)])
    mw_store.start()
    transform = (weights + mean_w).astype(BF16).reshape(block_dev * members, members)

    rr = iota((full, full), 0)
    cc = iota((full, full), 1)
    turn = one_hot((rr // block_dev == cc % members) & (rr % block_dev == cc // members))
    turned = dot(turn, transform).astype(BF16)
    repeat = one_hot(iota((full, members), 0) // block_dev == iota((full, members), 1))
    dense = dot_nt(repeat, turned)
    mix_mat[...] = jnp.where(rr % block_dev == cc % block_dev, dense, 0.0).astype(BF16)
    totals = dot(mix_mat[...], jnp.ones((full, width), BF16))
    gain_ref[...] = (1.0 - totals) * (1.0 / members)
    sum_mat = one_hot(iota((block_dev, full), 0) == iota((block_dev, full), 1) % block_dev)

    for g in range(groups):
        for k in peers:
            box_arrival(recv_box, fwd_send, fwd_recv, g, n - k).wait_recv()
        state = recv_box[g].reshape(full, width)
        product = dot(mix_mat[...], state).reshape(members, block_dev, width)
        member_sum = dot(sum_mat, state)
        gain = gain_ref[...].reshape(members, block_dev, width)
        analysis = (product + gain * member_sum[None]).astype(BF16)
        ret_box[g] = analysis.reshape(n, slab, width)
        back_box[g, pl.ds(me, 1)] = ret_box[g, pl.ds(me, 1)]
        for k in peers:
            box_copy(ret_box, back_box, bwd_send, bwd_recv, g, k).start()

    for g in range(groups):
        for k in peers:
            box_arrival(back_box, bwd_send, bwd_recv, g, n - k).wait_recv()
        final = dot(scatter_mat[...], back_box[g].reshape(full, width)).astype(BF16)
        for l in range(lev_group):
            for m in range(held):
                out_ref[m * LEV + g * lev_group + l] = final[
                    m * blocks : (m + 1) * blocks, l * points : (l + 1) * points
                ]
        for m in range(held):
            out_store(g, m).start()

    mw_store.wait()
    for g in range(groups):
        for m in range(held):
            out_store(g, m).wait()
    for k in peers:
        obs_copy(k).wait_send()
        for g in range(groups):
            box_copy(send_box, recv_box, fwd_send, fwd_recv, g, k).wait_send()
            box_copy(ret_box, back_box, bwd_send, bwd_recv, g, k).wait_send()


def fused(
    ensemble,
    owner_slot,
    weights,
    obs_members,
    departures,
    obs_count,
    pair_home,
    pair_index,
    localization,
    groups=2,
):
    n = lax.axis_size("grid")
    rows_here, blocks, points = ensemble.shape
    block_dev, members, _ = weights.shape
    held = rows_here // LEV
    slab = held * block_dev
    full = n * slab
    width = LEV // groups * points
    obs_dev = obs_members.shape[0]
    box = pltpu.VMEM((groups, n, slab, width), BF16)
    hbm = pl.BlockSpec(memory_space=pltpu.HBM)
    operands = (
        ensemble,
        owner_slot.reshape(1, blocks),
        weights,
        obs_members,
        departures,
        obs_count.reshape(1, obs_dev),
        pair_home.T,
        pair_index.T,
        localization,
    )
    return pl.pallas_call(
        functools.partial(fused_kernel, (n, groups)),
        out_shape=(
            jax.ShapeDtypeStruct(ensemble.shape, BF16),
            jax.ShapeDtypeStruct((block_dev, members), F32),
        ),
        in_specs=[hbm] * 9,
        out_specs=(hbm, hbm),
        scratch_shapes=[
            *[pltpu.VMEM(arg.shape, arg.dtype) for arg in operands],
            pltpu.VMEM(ensemble.shape, BF16),
            pltpu.VMEM((block_dev, members), F32),
            pltpu.VMEM((n, obs_dev // 2, LANES), BF16),
            box,
            box,
            box,
            box,
            pltpu.VMEM((full, full), BF16),
            pltpu.VMEM((full, full), BF16),
            pltpu.VMEM((full, full), BF16),
            pltpu.VMEM((full, width), F32),
            pltpu.SemaphoreType.DMA((len(operands),)),
            pltpu.SemaphoreType.DMA((groups, held)),
            pltpu.SemaphoreType.DMA((groups, held)),
            pltpu.SemaphoreType.DMA((n,)),
            pltpu.SemaphoreType.DMA((n,)),
            pltpu.SemaphoreType.DMA((groups, n)),
            pltpu.SemaphoreType.DMA((groups, n)),
            pltpu.SemaphoreType.DMA((groups, n)),
            pltpu.SemaphoreType.DMA((groups, n)),
        ],
        compiler_params=pltpu.CompilerParams(
            collective_id=0, has_side_effects=True, vmem_limit_bytes=48 * 2**20
        ),
    )(*operands)


def staged(
    ensemble,
    owner_slot,
    weights,
    obs_members,
    departures,
    obs_count,
    pair_home,
    pair_index,
    localization,
):
    devices = lax.axis_size("grid")
    my_index = lax.axis_index("grid")
    rows_here, blocks_all, points = ensemble.shape
    block_dev = weights.shape[0]
    members = weights.shape[1]
    pair_count = pair_home.shape[1]
    entries = block_dev * pair_count
    capacity = max(2, 2 * entries // devices)
    slot_pos = lax.broadcasted_iota(jnp.int32, departures.shape, 1)
    masked = jnp.where(slot_pos < obs_count[:, None], departures, jnp.zeros_like(departures))
    homes_all = pair_home.reshape(devices, entries)
    index_all = pair_index.reshape(devices, entries)
    matches = homes_all == my_index
    position = jnp.cumsum(matches.astype(jnp.int32), axis=1) - 1
    slot_ids = jnp.arange(capacity, dtype=jnp.int32)
    select = matches[:, None, :] & (position[:, None, :] == slot_ids[None, :, None])
    picked = jnp.sum(jnp.where(select, index_all[:, None, :], 0), axis=2)
    filled = jnp.any(select, axis=2)
    own_sums = jnp.einsum("okp,op->ok", obs_members, masked, preferred_element_type=jnp.float32)
    send_sums = jnp.where(filled[:, :, None], own_sums[picked], jnp.zeros((), jnp.float32))
    received = lax.all_to_all(send_sums, "grid", split_axis=0, concat_axis=0, tiled=True).reshape(
        devices * capacity, members
    )
    first_row = my_index * block_dev
    my_homes = lax.dynamic_slice_in_dim(pair_home, first_row, block_dev, 0).reshape(entries)
    order_row = lax.broadcasted_iota(jnp.int32, (entries, entries), 0)
    order_col = lax.broadcasted_iota(jnp.int32, (entries, entries), 1)
    earlier = (my_homes[:, None] == my_homes[None, :]) & (order_col < order_row)
    my_position = jnp.sum(earlier.astype(jnp.int32), axis=1)
    item_index = my_homes * capacity + my_position
    pair_sums = received[item_index].reshape(block_dev, pair_count, members)
    innovation = jnp.sum(localization[:, :, None] * pair_sums, axis=1)
    projected = jnp.einsum("bmi,bm->bi", weights, innovation, precision=lax.Precision.HIGHEST)
    mean_weights = jnp.einsum("bji,bi->bj", weights, projected, precision=lax.Precision.HIGHEST) / (
        members - 1
    )
    transform = (weights + mean_weights[:, :, None]).astype(jnp.bfloat16)
    column_totals = jnp.sum(transform.astype(jnp.float32), axis=1)
    inverse = (
        jnp.zeros((blocks_all,), jnp.int32)
        .at[owner_slot]
        .set(jnp.arange(blocks_all, dtype=jnp.int32))
    )
    ordered = ensemble[:, inverse, :]
    owned = lax.all_to_all(ordered, "grid", split_axis=1, concat_axis=0, tiled=True)
    states = owned.reshape(members, LEV, block_dev, points)
    ens_mean = jnp.sum(states, axis=0, dtype=jnp.float32) / members
    product = jnp.einsum("jlbp,bji->ilbp", states, transform, preferred_element_type=jnp.float32)
    analysis = (product + ens_mean[None] * (1.0 - column_totals).T[:, None, :, None]).astype(
        jnp.bfloat16
    )
    returned = lax.all_to_all(
        analysis.reshape(members * LEV, block_dev, points),
        "grid",
        split_axis=0,
        concat_axis=1,
        tiled=True,
    )
    result = returned[:, owner_slot, :]
    return (result, mean_weights)


def per_device(ensemble, owner_slot, weights, *rest):
    rows_here = ensemble.shape[0]
    block_dev = weights.shape[0]
    whole_members = rows_here % LEV == 0
    if whole_members and (rows_here // LEV) * block_dev % 16 == 0:
        return fused(ensemble, owner_slot, weights, *rest)
    return staged(ensemble, owner_slot, weights, *rest)


def solution(mesh):
    placed = (
        P(("groups", "grid"), None, None),
        P("groups"),
        P(("groups", "grid"), None, None),
        P(("groups", "grid"), None, None),
        P(("groups", "grid"), None),
        P(("groups", "grid")),
        P("groups", None),
        P("groups", None),
        P(("groups", "grid"), None),
    )
    return jax.shard_map(
        per_device,
        mesh=mesh,
        in_specs=placed,
        out_specs=(P(("groups", "grid"), None, None), P(("groups", "grid"), None)),
        check_vma=False,
    )
```

```python
import functools

import jax
import jax.numpy as jnp
from jax import lax
from jax.experimental import pallas as pl
from jax.experimental.pallas import tpu as pltpu
from jax.sharding import PartitionSpec as P

LEV = 8
LANES = 128
F32 = jnp.float32
BF16 = jnp.bfloat16
HIGHEST = lax.Precision.HIGHEST


def iota(shape, dim):
    return lax.broadcasted_iota(jnp.int32, shape, dim)


def one_hot(cond):
    return jnp.where(cond, 1.0, 0.0).astype(BF16)


def dot(a, b):
    return jnp.dot(a, b, preferred_element_type=F32)


def dot_nt(a, b, precision=None):
    return lax.dot_general(
        a, b, (((1,), (1,)), ((), ())), preferred_element_type=F32, precision=precision
    )


def peer_order(n):
    return list(range(1, n))


def fused_kernel(
    dims,
    ens_hbm,
    owner_hbm,
    weights_hbm,
    obs_hbm,
    dep_hbm,
    count_hbm,
    home_hbm,
    index_hbm,
    loc_hbm,
    out_hbm,
    mw_hbm,
    ens_ref,
    owner_ref,
    weights_ref,
    obs_ref,
    dep_ref,
    count_ref,
    home_ref,
    index_ref,
    loc_ref,
    out_ref,
    mw_ref,
    obs_box,
    send_box,
    recv_box,
    ret_box,
    back_box,
    gather_mat,
    scatter_mat,
    mix_mat,
    gain_ref,
    load_sem,
    ens_sem,
    out_sem,
    obs_send,
    obs_recv,
    fwd_send,
    fwd_recv,
    bwd_send,
    bwd_recv,
):
    n, groups = dims
    me = lax.axis_index("grid")
    rows_here, blocks, points = ens_ref.shape
    block_dev, members, _ = weights_ref.shape
    obs_dev = obs_ref.shape[0]
    pair_count = home_ref.shape[0]
    held = rows_here // LEV
    slab = held * block_dev
    full = n * slab
    lev_group = LEV // groups
    width = lev_group * points
    packed = obs_dev // 2
    peers = peer_order(n)

    barrier = pltpu.get_barrier_semaphore()
    for k in peers:
        pl.semaphore_signal(
            barrier,
            inc=1,
            device_id={"grid": lax.rem(me + k, n)},
            device_id_type=pl.DeviceIdType.MESH,
        )

    def level_rows(g, m):
        return pl.ds(m * LEV + g * lev_group, lev_group)

    def ens_load(g, m):
        rows = level_rows(g, m)
        return pltpu.make_async_copy(ens_hbm.at[rows], ens_ref.at[rows], ens_sem.at[g, m])

    def out_store(g, m):
        rows = level_rows(g, m)
        return pltpu.make_async_copy(out_ref.at[rows], out_hbm.at[rows], out_sem.at[g, m])

    small = (
        (owner_hbm, owner_ref),
        (obs_hbm, obs_ref),
        (dep_hbm, dep_ref),
        (count_hbm, count_ref),
        (home_hbm, home_ref),
        (index_hbm, index_ref),
        (loc_hbm, loc_ref),
        (weights_hbm, weights_ref),
    )
    loads = [
        pltpu.make_async_copy(src, dst, load_sem.at[i]) for i, (src, dst) in enumerate(small)
    ]
    loads[0].start()
    for g in range(groups):
        for m in range(held):
            ens_load(g, m).start()
    for load in loads[1:]:
        load.start()

    r = iota((full, 1), 0)
    row_key = (r // block_dev % held) * blocks + (r // slab) * block_dev + r % block_dev
    loads[0].wait()
    owner = jnp.concatenate([owner_ref[...]] * held, axis=1)
    col_key = owner + iota((1, full), 1) // blocks * blocks
    gather_mat[...] = one_hot(row_key == col_key)

    def arrange(g):
        for m in range(held):
            ens_load(g, m).wait()
        cols = []
        for l in range(g * lev_group, (g + 1) * lev_group):
            cols.append(
                jnp.concatenate([ens_ref[m * LEV + l] for m in range(held)], axis=0)
            )
        state = jnp.concatenate(cols, axis=1)
        sorted_state = dot(gather_mat[...], state).astype(BF16)
        send_box[g] = sorted_state.reshape(n, slab, width)
        recv_box[g, pl.ds(me, 1)] = send_box[g, pl.ds(me, 1)]

    def obs_copy(k):
        to = lax.rem(me + k, n)
        return pltpu.make_async_remote_copy(
            src_ref=obs_box.at[me],
            dst_ref=obs_box.at[me],
            send_sem=obs_send.at[k],
            recv_sem=obs_recv.at[me],
            device_id={"grid": to},
            device_id_type=pl.DeviceIdType.MESH,
        )

    def box_copy(src, dst, send_sem, recv_sem, g, k):
        to = lax.rem(me + k, n)
        return pltpu.make_async_remote_copy(
            src_ref=src.at[g, to],
            dst_ref=dst.at[g, me],
            send_sem=send_sem.at[g, k],
            recv_sem=recv_sem.at[g, me],
            device_id={"grid": to},
            device_id_type=pl.DeviceIdType.MESH,
        )

    def box_arrival(dst, send_sem, recv_sem, g, k):
        src = lax.rem(me + k, n)
        return pltpu.make_async_remote_copy(
            src_ref=dst.at[g, src],
            dst_ref=dst.at[g, src],
            send_sem=send_sem.at[g, k],
            recv_sem=recv_sem.at[g, src],
            device_id={"grid": src},
            device_id_type=pl.DeviceIdType.MESH,
        )

    arrange(0)
    pl.semaphore_wait(barrier, n - 1)
    for k in peers:
        box_copy(send_box, recv_box, fwd_send, fwd_recv, 0, k).start()

    for load in loads[1:]:
        load.wait()
    lane = iota((obs_dev, points), 1)
    dep = dep_ref[...].astype(F32)
    square = iota((obs_dev, obs_dev), 0) == iota((obs_dev, obs_dev), 1)
    count = jnp.sum(jnp.where(square, count_ref[...], 0), axis=1, keepdims=True)
    masked = jnp.where(lane < count, dep, 0.0).astype(BF16)
    cross = dot_nt(masked, obs_ref[...].reshape(obs_dev * members, points))
    row = iota((obs_dev, LANES), 0)
    lane_block = iota((obs_dev, LANES), 1) // members
    per_row = LANES // members
    sums = jnp.zeros((obs_dev, LANES), F32)
    for t in range(obs_dev * members // LANES):
        piece = cross[:, t * LANES : (t + 1) * LANES]
        sums = sums + jnp.where(row == lane_block + t * per_row, piece, 0.0)
    fold = one_hot(iota((packed, obs_dev), 0) == iota((packed, obs_dev), 1) // 2)
    obs_box[pl.ds(me, 1)] = dot(fold, sums.astype(BF16)).astype(BF16)[None]

    for k in peers:
        obs_copy(k).start()
    for g in range(1, groups):
        arrange(g)
        for k in peers:
            box_copy(send_box, recv_box, fwd_send, fwd_recv, g, k).start()

    same = one_hot(iota((full, full), 0) == iota((full, full), 1))
    scatter_mat[...] = dot_nt(same, gather_mat[...]).astype(BF16)

    for k in peers:
        src = lax.rem(me + k, n)
        pltpu.make_async_remote_copy(
            src_ref=obs_box.at[src],
            dst_ref=obs_box.at[src],
            send_sem=obs_send.at[k],
            recv_sem=obs_recv.at[src],
            device_id={"grid": src},
            device_id_type=pl.DeviceIdType.MESH,
        ).wait_recv()
    all_sums = obs_box[...].reshape(n * packed, LANES).astype(F32)
    mine = one_hot(
        iota((block_dev, blocks), 1) == iota((block_dev, blocks), 0) + me * block_dev
    )
    home = dot_nt(mine, home_ref[...].astype(F32).astype(BF16)).astype(jnp.int32)
    index = dot_nt(mine, index_ref[...].astype(F32).astype(BF16)).astype(jnp.int32)
    spot = home * packed + index // 2
    odd = index % 2
    loc = loc_ref[...]
    col = iota((block_dev, n * packed), 1)
    pick = [jnp.zeros((block_dev, n * packed), F32) for _ in range(2)]
    for k in range(pair_count):
        hit = col == spot[:, k : k + 1]
        for parity in range(2):
            gate = jnp.where(odd[:, k : k + 1] == parity, loc[:, k : k + 1], 0.0)
            pick[parity] = pick[parity] + jnp.where(hit, gate, 0.0)
    even_part = jnp.dot(pick[0], all_sums, precision=HIGHEST, preferred_element_type=F32)
    odd_part = jnp.dot(pick[1], all_sums, precision=HIGHEST, preferred_element_type=F32)
    innovation = even_part[:, :members] + odd_part[:, members:]

    weights = weights_ref[...]
    flat = weights.reshape(block_dev * members, members)
    twice = jnp.concatenate([innovation, innovation], axis=1)
    spread = jnp.concatenate([twice] * (block_dev // 2), axis=1)
    spread_row = iota((block_dev, block_dev * members), 0)
    spread_col = iota((block_dev, block_dev * members), 1) // members
    spread = jnp.where(spread_row == spread_col, spread, 0.0)
    projected = jnp.dot(spread, flat, precision=HIGHEST, preferred_element_type=F32)
    mean_w = jnp.sum(weights * projected[:, None, :], axis=2, keepdims=True) / (members - 1)
    mw_ref[...] = jnp.sum(weights * projected[:, None, :], axis=2) / (members - 1)
    mw_store = pltpu.make_async_copy(mw_ref, mw_hbm, load_sem.at[len(loads)])
    mw_store.start()
    transform = (weights + mean_w).astype(BF16).reshape(block_dev * members, members)

    rr = iota((full, full), 0)
    cc = iota((full, full), 1)
    turn = one_hot((rr // block_dev == cc % members) & (rr % block_dev == cc // members))
    turned = dot(turn, transform).astype(BF16)
    repeat = one_hot(iota((full, members), 0) // block_dev == iota((full, members), 1))
    dense = dot_nt(repeat, turned)
    mix_mat[...] = jnp.where(rr % block_dev == cc % block_dev, dense, 0.0).astype(BF16)
    totals = dot(mix_mat[...], jnp.ones((full, width), BF16))
    gain_ref[...] = (1.0 - totals) * (1.0 / members)
    sum_mat = one_hot(iota((block_dev, full), 0) == iota((block_dev, full), 1) % block_dev)

    for g in range(groups):
        for k in peers:
            box_arrival(recv_box, fwd_send, fwd_recv, g, n - k).wait_recv()
        state = recv_box[g].reshape(full, width)
        product = dot(mix_mat[...], state).reshape(members, block_dev, width)
        member_sum = dot(sum_mat, state)
        gain = gain_ref[...].reshape(members, block_dev, width)
        analysis = (product + gain * member_sum[None]).astype(BF16)
        ret_box[g] = analysis.reshape(n, slab, width)
        back_box[g, pl.ds(me, 1)] = ret_box[g, pl.ds(me, 1)]
        for k in peers:
            box_copy(ret_box, back_box, bwd_send, bwd_recv, g, k).start()

    for g in range(groups):
        for k in peers:
            box_arrival(back_box, bwd_send, bwd_recv, g, n - k).wait_recv()
        final = dot(scatter_mat[...], back_box[g].reshape(full, width)).astype(BF16)
        for l in range(lev_group):
            for m in range(held):
                out_ref[m * LEV + g * lev_group + l] = final[
                    m * blocks : (m + 1) * blocks, l * points : (l + 1) * points
                ]
        for m in range(held):
            out_store(g, m).start()

    mw_store.wait()
    for g in range(groups):
        for m in range(held):
            out_store(g, m).wait()
    for k in peers:
        obs_copy(k).wait_send()
        for g in range(groups):
            box_copy(send_box, recv_box, fwd_send, fwd_recv, g, k).wait_send()
            box_copy(ret_box, back_box, bwd_send, bwd_recv, g, k).wait_send()


def fused(
    ensemble,
    owner_slot,
    weights,
    obs_members,
    departures,
    obs_count,
    pair_home,
    pair_index,
    localization,
    groups=2,
):
    n = lax.axis_size("grid")
    rows_here, blocks, points = ensemble.shape
    block_dev, members, _ = weights.shape
    held = rows_here // LEV
    slab = held * block_dev
    full = n * slab
    width = LEV // groups * points
    obs_dev = obs_members.shape[0]
    box = pltpu.VMEM((groups, n, slab, width), BF16)
    hbm = pl.BlockSpec(memory_space=pltpu.HBM)
    operands = (
        ensemble,
        owner_slot.reshape(1, blocks),
        weights,
        obs_members,
        departures,
        obs_count.reshape(1, obs_dev),
        pair_home.T,
        pair_index.T,
        localization,
    )
    return pl.pallas_call(
        functools.partial(fused_kernel, (n, groups)),
        out_shape=(
            jax.ShapeDtypeStruct(ensemble.shape, BF16),
            jax.ShapeDtypeStruct((block_dev, members), F32),
        ),
        in_specs=[hbm] * 9,
        out_specs=(hbm, hbm),
        scratch_shapes=[
            *[pltpu.VMEM(arg.shape, arg.dtype) for arg in operands],
            pltpu.VMEM(ensemble.shape, BF16),
            pltpu.VMEM((block_dev, members), F32),
            pltpu.VMEM((n, obs_dev // 2, LANES), BF16),
            box,
            box,
            box,
            box,
            pltpu.VMEM((full, full), BF16),
            pltpu.VMEM((full, full), BF16),
            pltpu.VMEM((full, full), BF16),
            pltpu.VMEM((full, width), F32),
            pltpu.SemaphoreType.DMA((len(operands),)),
            pltpu.SemaphoreType.DMA((groups, held)),
            pltpu.SemaphoreType.DMA((groups, held)),
            pltpu.SemaphoreType.DMA((n,)),
            pltpu.SemaphoreType.DMA((n,)),
            pltpu.SemaphoreType.DMA((groups, n)),
            pltpu.SemaphoreType.DMA((groups, n)),
            pltpu.SemaphoreType.DMA((groups, n)),
            pltpu.SemaphoreType.DMA((groups, n)),
        ],
        compiler_params=pltpu.CompilerParams(
            collective_id=0, has_side_effects=True, vmem_limit_bytes=60 * 2**20
        ),
    )(*operands)


def staged(
    ensemble,
    owner_slot,
    weights,
    obs_members,
    departures,
    obs_count,
    pair_home,
    pair_index,
    localization,
):
    devices = lax.axis_size("grid")
    my_index = lax.axis_index("grid")
    rows_here, blocks_all, points = ensemble.shape
    block_dev = weights.shape[0]
    members = weights.shape[1]
    pair_count = pair_home.shape[1]
    entries = block_dev * pair_count
    capacity = max(2, 2 * entries // devices)
    slot_pos = lax.broadcasted_iota(jnp.int32, departures.shape, 1)
    masked = jnp.where(slot_pos < obs_count[:, None], departures, jnp.zeros_like(departures))
    homes_all = pair_home.reshape(devices, entries)
    index_all = pair_index.reshape(devices, entries)
    matches = homes_all == my_index
    position = jnp.cumsum(matches.astype(jnp.int32), axis=1) - 1
    slot_ids = jnp.arange(capacity, dtype=jnp.int32)
    select = matches[:, None, :] & (position[:, None, :] == slot_ids[None, :, None])
    picked = jnp.sum(jnp.where(select, index_all[:, None, :], 0), axis=2)
    filled = jnp.any(select, axis=2)
    own_sums = jnp.einsum("okp,op->ok", obs_members, masked, preferred_element_type=jnp.float32)
    send_sums = jnp.where(filled[:, :, None], own_sums[picked], jnp.zeros((), jnp.float32))
    received = lax.all_to_all(send_sums, "grid", split_axis=0, concat_axis=0, tiled=True).reshape(
        devices * capacity, members
    )
    first_row = my_index * block_dev
    my_homes = lax.dynamic_slice_in_dim(pair_home, first_row, block_dev, 0).reshape(entries)
    order_row = lax.broadcasted_iota(jnp.int32, (entries, entries), 0)
    order_col = lax.broadcasted_iota(jnp.int32, (entries, entries), 1)
    earlier = (my_homes[:, None] == my_homes[None, :]) & (order_col < order_row)
    my_position = jnp.sum(earlier.astype(jnp.int32), axis=1)
    item_index = my_homes * capacity + my_position
    pair_sums = received[item_index].reshape(block_dev, pair_count, members)
    innovation = jnp.sum(localization[:, :, None] * pair_sums, axis=1)
    projected = jnp.einsum("bmi,bm->bi", weights, innovation, precision=lax.Precision.HIGHEST)
    mean_weights = jnp.einsum("bji,bi->bj", weights, projected, precision=lax.Precision.HIGHEST) / (
        members - 1
    )
    transform = (weights + mean_weights[:, :, None]).astype(jnp.bfloat16)
    column_totals = jnp.sum(transform.astype(jnp.float32), axis=1)
    inverse = (
        jnp.zeros((blocks_all,), jnp.int32)
        .at[owner_slot]
        .set(jnp.arange(blocks_all, dtype=jnp.int32))
    )
    ordered = ensemble[:, inverse, :]
    owned = lax.all_to_all(ordered, "grid", split_axis=1, concat_axis=0, tiled=True)
    states = owned.reshape(members, LEV, block_dev, points)
    ens_mean = jnp.sum(states, axis=0, dtype=jnp.float32) / members
    product = jnp.einsum("jlbp,bji->ilbp", states, transform, preferred_element_type=jnp.float32)
    analysis = (product + ens_mean[None] * (1.0 - column_totals).T[:, None, :, None]).astype(
        jnp.bfloat16
    )
    returned = lax.all_to_all(
        analysis.reshape(members * LEV, block_dev, points),
        "grid",
        split_axis=0,
        concat_axis=1,
        tiled=True,
    )
    result = returned[:, owner_slot, :]
    return (result, mean_weights)


def per_device(ensemble, owner_slot, weights, *rest):
    rows_here = ensemble.shape[0]
    block_dev = weights.shape[0]
    whole_members = rows_here % LEV == 0
    if whole_members and (rows_here // LEV) * block_dev % 16 == 0:
        return fused(ensemble, owner_slot, weights, *rest)
    return staged(ensemble, owner_slot, weights, *rest)


def solution(mesh):
    placed = (
        P(("groups", "grid"), None, None),
        P("groups"),
        P(("groups", "grid"), None, None),
        P(("groups", "grid"), None, None),
        P(("groups", "grid"), None),
        P(("groups", "grid")),
        P("groups", None),
        P("groups", None),
        P(("groups", "grid"), None),
    )
    return jax.shard_map(
        per_device,
        mesh=mesh,
        in_specs=placed,
        out_specs=(P(("groups", "grid"), None, None), P(("groups", "grid"), None)),
        check_vma=False,
    )
```

```python
import functools

import jax
import jax.numpy as jnp
from jax import lax
from jax.experimental import pallas as pl
from jax.experimental.pallas import tpu as pltpu
from jax.sharding import PartitionSpec as P

LEV = 8
LANES = 128
F32 = jnp.float32
BF16 = jnp.bfloat16
HIGHEST = lax.Precision.HIGHEST


def iota(shape, dim):
    return lax.broadcasted_iota(jnp.int32, shape, dim)


def one_hot(cond):
    return jnp.where(cond, 1.0, 0.0).astype(BF16)


def dot(a, b):
    return jnp.dot(a, b, preferred_element_type=F32)


def dot_nt(a, b, precision=None):
    return lax.dot_general(
        a, b, (((1,), (1,)), ((), ())), preferred_element_type=F32, precision=precision
    )


def peer_order(n):
    return list(range(1, n))


def fused_kernel(
    dims,
    ens_hbm,
    owner_hbm,
    weights_hbm,
    obs_hbm,
    dep_hbm,
    count_hbm,
    home_hbm,
    index_hbm,
    loc_hbm,
    back_box,
    scatter_hbm,
    mw_hbm,
    ens_ref,
    owner_ref,
    weights_ref,
    obs_ref,
    dep_ref,
    count_ref,
    home_ref,
    index_ref,
    loc_ref,
    mw_ref,
    obs_box,
    send_box,
    recv_box,
    ret_box,
    gather_mat,
    scatter_mat,
    mix_mat,
    gain_ref,
    load_sem,
    ens_sem,
    own_sem,
    obs_send,
    obs_recv,
    fwd_send,
    fwd_recv,
    bwd_send,
    bwd_recv,
):
    n, groups = dims
    me = lax.axis_index("grid")
    rows_here, blocks, points = ens_ref.shape
    block_dev, members, _ = weights_ref.shape
    obs_dev = obs_ref.shape[0]
    pair_count = home_ref.shape[0]
    held = rows_here // LEV
    slab = held * block_dev
    full = n * slab
    lev_group = LEV // groups
    width = lev_group * points
    packed = obs_dev // 2
    peers = peer_order(n)

    barrier = pltpu.get_barrier_semaphore()
    for k in peers:
        pl.semaphore_signal(
            barrier,
            inc=1,
            device_id={"grid": lax.rem(me + k, n)},
            device_id_type=pl.DeviceIdType.MESH,
        )

    def level_rows(g, m):
        return pl.ds(m * LEV + g * lev_group, lev_group)

    def ens_load(g, m):
        rows = level_rows(g, m)
        return pltpu.make_async_copy(ens_hbm.at[rows], ens_ref.at[rows], ens_sem.at[g, m])

    def own_return(g):
        return pltpu.make_async_copy(ret_box.at[g, me], back_box.at[g, me], own_sem.at[g])

    small = (
        (owner_hbm, owner_ref),
        (obs_hbm, obs_ref),
        (dep_hbm, dep_ref),
        (count_hbm, count_ref),
        (home_hbm, home_ref),
        (index_hbm, index_ref),
        (loc_hbm, loc_ref),
        (weights_hbm, weights_ref),
    )
    loads = [
        pltpu.make_async_copy(src, dst, load_sem.at[i]) for i, (src, dst) in enumerate(small)
    ]
    loads[0].start()
    for g in range(groups):
        for m in range(held):
            ens_load(g, m).start()
    for load in loads[1:]:
        load.start()

    r = iota((full, 1), 0)
    row_key = (r // block_dev % held) * blocks + (r // slab) * block_dev + r % block_dev
    loads[0].wait()
    owner = jnp.concatenate([owner_ref[...]] * held, axis=1)
    col_key = owner + iota((1, full), 1) // blocks * blocks
    gather_mat[...] = one_hot(row_key == col_key)

    def arrange(g):
        for m in range(held):
            ens_load(g, m).wait()
        cols = []
        for l in range(g * lev_group, (g + 1) * lev_group):
            cols.append(
                jnp.concatenate([ens_ref[m * LEV + l] for m in range(held)], axis=0)
            )
        state = jnp.concatenate(cols, axis=1)
        sorted_state = dot(gather_mat[...], state).astype(BF16)
        send_box[g] = sorted_state.reshape(n, slab, width)
        recv_box[g, pl.ds(me, 1)] = send_box[g, pl.ds(me, 1)]

    def obs_copy(k):
        to = lax.rem(me + k, n)
        return pltpu.make_async_remote_copy(
            src_ref=obs_box.at[me],
            dst_ref=obs_box.at[me],
            send_sem=obs_send.at[k],
            recv_sem=obs_recv.at[me],
            device_id={"grid": to},
            device_id_type=pl.DeviceIdType.MESH,
        )

    def box_copy(src, dst, send_sem, recv_sem, g, k):
        to = lax.rem(me + k, n)
        return pltpu.make_async_remote_copy(
            src_ref=src.at[g, to],
            dst_ref=dst.at[g, me],
            send_sem=send_sem.at[g, k],
            recv_sem=recv_sem.at[g, me],
            device_id={"grid": to},
            device_id_type=pl.DeviceIdType.MESH,
        )

    def box_arrival(dst, send_sem, recv_sem, g, k):
        src = lax.rem(me + k, n)
        return pltpu.make_async_remote_copy(
            src_ref=dst.at[g, src],
            dst_ref=dst.at[g, src],
            send_sem=send_sem.at[g, k],
            recv_sem=recv_sem.at[g, src],
            device_id={"grid": src},
            device_id_type=pl.DeviceIdType.MESH,
        )

    arrange(0)
    pl.semaphore_wait(barrier, n - 1)
    for k in peers:
        box_copy(send_box, recv_box, fwd_send, fwd_recv, 0, k).start()

    for load in loads[1:]:
        load.wait()
    lane = iota((obs_dev, points), 1)
    dep = dep_ref[...].astype(F32)
    square = iota((obs_dev, obs_dev), 0) == iota((obs_dev, obs_dev), 1)
    count = jnp.sum(jnp.where(square, count_ref[...], 0), axis=1, keepdims=True)
    masked = jnp.where(lane < count, dep, 0.0).astype(BF16)
    cross = dot_nt(masked, obs_ref[...].reshape(obs_dev * members, points))
    row = iota((obs_dev, LANES), 0)
    lane_block = iota((obs_dev, LANES), 1) // members
    per_row = LANES // members
    sums = jnp.zeros((obs_dev, LANES), F32)
    for t in range(obs_dev * members // LANES):
        piece = cross[:, t * LANES : (t + 1) * LANES]
        sums = sums + jnp.where(row == lane_block + t * per_row, piece, 0.0)
    fold = one_hot(iota((packed, obs_dev), 0) == iota((packed, obs_dev), 1) // 2)
    obs_box[pl.ds(me, 1)] = dot(fold, sums.astype(BF16)).astype(BF16)[None]

    for k in peers:
        obs_copy(k).start()
    for g in range(1, groups):
        arrange(g)
        for k in peers:
            box_copy(send_box, recv_box, fwd_send, fwd_recv, g, k).start()

    same = one_hot(iota((full, full), 0) == iota((full, full), 1))
    scatter_mat[...] = dot_nt(same, gather_mat[...]).astype(BF16)
    scatter_store = pltpu.make_async_copy(scatter_mat, scatter_hbm, load_sem.at[len(loads)])
    scatter_store.start()

    for k in peers:
        src = lax.rem(me + k, n)
        pltpu.make_async_remote_copy(
            src_ref=obs_box.at[src],
            dst_ref=obs_box.at[src],
            send_sem=obs_send.at[k],
            recv_sem=obs_recv.at[src],
            device_id={"grid": src},
            device_id_type=pl.DeviceIdType.MESH,
        ).wait_recv()
    all_sums = obs_box[...].reshape(n * packed, LANES).astype(F32)
    mine = one_hot(
        iota((block_dev, blocks), 1) == iota((block_dev, blocks), 0) + me * block_dev
    )
    home = dot_nt(mine, home_ref[...].astype(F32).astype(BF16)).astype(jnp.int32)
    index = dot_nt(mine, index_ref[...].astype(F32).astype(BF16)).astype(jnp.int32)
    spot = home * packed + index // 2
    odd = index % 2
    loc = loc_ref[...]
    col = iota((block_dev, n * packed), 1)
    pick = [jnp.zeros((block_dev, n * packed), F32) for _ in range(2)]
    for k in range(pair_count):
        hit = col == spot[:, k : k + 1]
        for parity in range(2):
            gate = jnp.where(odd[:, k : k + 1] == parity, loc[:, k : k + 1], 0.0)
            pick[parity] = pick[parity] + jnp.where(hit, gate, 0.0)
    even_part = jnp.dot(pick[0], all_sums, precision=HIGHEST, preferred_element_type=F32)
    odd_part = jnp.dot(pick[1], all_sums, precision=HIGHEST, preferred_element_type=F32)
    innovation = even_part[:, :members] + odd_part[:, members:]

    weights = weights_ref[...]
    flat = weights.reshape(block_dev * members, members)
    twice = jnp.concatenate([innovation, innovation], axis=1)
    spread = jnp.concatenate([twice] * (block_dev // 2), axis=1)
    spread_row = iota((block_dev, block_dev * members), 0)
    spread_col = iota((block_dev, block_dev * members), 1) // members
    spread = jnp.where(spread_row == spread_col, spread, 0.0)
    projected = jnp.dot(spread, flat, precision=HIGHEST, preferred_element_type=F32)
    mean_w = jnp.sum(weights * projected[:, None, :], axis=2, keepdims=True) / (members - 1)
    mw_ref[...] = jnp.sum(weights * projected[:, None, :], axis=2) / (members - 1)
    mw_store = pltpu.make_async_copy(mw_ref, mw_hbm, load_sem.at[len(loads) + 1])
    mw_store.start()
    transform = (weights + mean_w).astype(BF16).reshape(block_dev * members, members)

    rr = iota((full, full), 0)
    cc = iota((full, full), 1)
    turn = one_hot((rr // block_dev == cc % members) & (rr % block_dev == cc // members))
    turned = dot(turn, transform).astype(BF16)
    repeat = one_hot(iota((full, members), 0) // block_dev == iota((full, members), 1))
    dense = dot_nt(repeat, turned)
    mix_mat[...] = jnp.where(rr % block_dev == cc % block_dev, dense, 0.0).astype(BF16)
    totals = dot(mix_mat[...], jnp.ones((full, width), BF16))
    gain_ref[...] = (1.0 - totals) * (1.0 / members)
    sum_mat = one_hot(iota((block_dev, full), 0) == iota((block_dev, full), 1) % block_dev)

    for g in range(groups):
        for k in peers:
            box_arrival(recv_box, fwd_send, fwd_recv, g, n - k).wait_recv()
        state = recv_box[g].reshape(full, width)
        product = dot(mix_mat[...], state).reshape(members, block_dev, width)
        member_sum = dot(sum_mat, state)
        gain = gain_ref[...].reshape(members, block_dev, width)
        analysis = (product + gain * member_sum[None]).astype(BF16)
        ret_box[g] = analysis.reshape(n, slab, width)
        own_return(g).start()
        for k in peers:
            box_copy(ret_box, back_box, bwd_send, bwd_recv, g, k).start()

    for k in peers:
        obs_copy(k).wait_send()
        for g in range(groups):
            box_copy(send_box, recv_box, fwd_send, fwd_recv, g, k).wait_send()
            box_copy(ret_box, back_box, bwd_send, bwd_recv, g, k).wait_send()
    scatter_store.wait()
    mw_store.wait()
    for g in range(groups):
        own_return(g).wait()
        for k in peers:
            box_arrival(back_box, bwd_send, bwd_recv, g, n - k).wait_recv()


def restore_kernel(
    back_hbm,
    scatter_hbm,
    mw_hbm,
    out_hbm,
    mw_out,
    back_ref,
    scatter_ref,
    mw_ref,
    out_ref,
    fixed_sem,
    in_sem,
    out_sem,
):
    groups, n, slab, width = back_ref.shape
    held, _, blocks, points = out_ref.shape
    lev_group = width // points
    scatter_load = pltpu.make_async_copy(scatter_hbm, scatter_ref, fixed_sem.at[0])
    mw_load = pltpu.make_async_copy(mw_hbm, mw_ref, fixed_sem.at[1])
    mw_store = pltpu.make_async_copy(mw_ref, mw_out, fixed_sem.at[2])

    def load(g):
        return pltpu.make_async_copy(back_hbm.at[g], back_ref.at[g], in_sem.at[g])

    def store(l):
        return pltpu.make_async_copy(out_ref.at[:, l], out_hbm.at[:, l], out_sem.at[l])

    scatter_load.start()
    for g in range(groups):
        load(g).start()
    mw_load.start()
    mw_load.wait()
    mw_store.start()
    scatter_load.wait()
    step = 2 * points
    for g in range(groups):
        load(g).wait()
        for c in range(width // step):
            state = back_ref[g, :, :, c * step : (c + 1) * step].reshape(n * slab, step)
            final = dot(scatter_ref[...], state).astype(BF16)
            for t in range(2):
                l = g * lev_group + c * 2 + t
                for m in range(held):
                    out_ref[m, l] = final[
                        m * blocks : (m + 1) * blocks, t * points : (t + 1) * points
                    ]
                store(l).start()
    mw_store.wait()
    for l in range(LEV):
        store(l).wait()


def fused(
    ensemble,
    owner_slot,
    weights,
    obs_members,
    departures,
    obs_count,
    pair_home,
    pair_index,
    localization,
    groups=2,
):
    n = lax.axis_size("grid")
    rows_here, blocks, points = ensemble.shape
    block_dev, members, _ = weights.shape
    held = rows_here // LEV
    slab = held * block_dev
    full = n * slab
    width = LEV // groups * points
    obs_dev = obs_members.shape[0]
    box = pltpu.VMEM((groups, n, slab, width), BF16)
    hbm = pl.BlockSpec(memory_space=pltpu.HBM)
    operands = (
        ensemble,
        owner_slot.reshape(1, blocks),
        weights,
        obs_members,
        departures,
        obs_count.reshape(1, obs_dev),
        pair_home.T,
        pair_index.T,
        localization,
    )
    back, scatter, mean_weights = pl.pallas_call(
        functools.partial(fused_kernel, (n, groups)),
        out_shape=(
            jax.ShapeDtypeStruct((groups, n, slab, width), BF16),
            jax.ShapeDtypeStruct((full, full), BF16),
            jax.ShapeDtypeStruct((block_dev, members), F32),
        ),
        in_specs=[hbm] * 9,
        out_specs=(hbm, hbm, hbm),
        scratch_shapes=[
            *[pltpu.VMEM(arg.shape, arg.dtype) for arg in operands],
            pltpu.VMEM((block_dev, members), F32),
            pltpu.VMEM((n, obs_dev // 2, LANES), BF16),
            box,
            box,
            box,
            pltpu.VMEM((full, full), BF16),
            pltpu.VMEM((full, full), BF16),
            pltpu.VMEM((full, full), BF16),
            pltpu.VMEM((full, width), F32),
            pltpu.SemaphoreType.DMA((len(operands) + 1,)),
            pltpu.SemaphoreType.DMA((groups, held)),
            pltpu.SemaphoreType.DMA((groups,)),
            pltpu.SemaphoreType.DMA((n,)),
            pltpu.SemaphoreType.DMA((n,)),
            pltpu.SemaphoreType.DMA((groups, n)),
            pltpu.SemaphoreType.DMA((groups, n)),
            pltpu.SemaphoreType.DMA((groups, n)),
            pltpu.SemaphoreType.DMA((groups, n)),
        ],
        compiler_params=pltpu.CompilerParams(
            collective_id=0, has_side_effects=True, vmem_limit_bytes=60 * 2**20
        ),
    )(*operands)
    analysis, mean_weights = pl.pallas_call(
        restore_kernel,
        out_shape=(
            jax.ShapeDtypeStruct((held, LEV, blocks, points), BF16),
            jax.ShapeDtypeStruct((block_dev, members), F32),
        ),
        in_specs=[hbm] * 3,
        out_specs=(hbm, hbm),
        scratch_shapes=[
            pltpu.VMEM((groups, n, slab, width), BF16),
            pltpu.VMEM((full, full), BF16),
            pltpu.VMEM((block_dev, members), F32),
            pltpu.VMEM((held, LEV, blocks, points), BF16),
            pltpu.SemaphoreType.DMA((3,)),
            pltpu.SemaphoreType.DMA((groups,)),
            pltpu.SemaphoreType.DMA((LEV,)),
        ],
        compiler_params=pltpu.CompilerParams(vmem_limit_bytes=60 * 2**20),
    )(back, scatter, mean_weights)
    return analysis.reshape(ensemble.shape), mean_weights


def staged(
    ensemble,
    owner_slot,
    weights,
    obs_members,
    departures,
    obs_count,
    pair_home,
    pair_index,
    localization,
):
    devices = lax.axis_size("grid")
    my_index = lax.axis_index("grid")
    rows_here, blocks_all, points = ensemble.shape
    block_dev = weights.shape[0]
    members = weights.shape[1]
    pair_count = pair_home.shape[1]
    entries = block_dev * pair_count
    capacity = max(2, 2 * entries // devices)
    slot_pos = lax.broadcasted_iota(jnp.int32, departures.shape, 1)
    masked = jnp.where(slot_pos < obs_count[:, None], departures, jnp.zeros_like(departures))
    homes_all = pair_home.reshape(devices, entries)
    index_all = pair_index.reshape(devices, entries)
    matches = homes_all == my_index
    position = jnp.cumsum(matches.astype(jnp.int32), axis=1) - 1
    slot_ids = jnp.arange(capacity, dtype=jnp.int32)
    select = matches[:, None, :] & (position[:, None, :] == slot_ids[None, :, None])
    picked = jnp.sum(jnp.where(select, index_all[:, None, :], 0), axis=2)
    filled = jnp.any(select, axis=2)
    own_sums = jnp.einsum("okp,op->ok", obs_members, masked, preferred_element_type=jnp.float32)
    send_sums = jnp.where(filled[:, :, None], own_sums[picked], jnp.zeros((), jnp.float32))
    received = lax.all_to_all(send_sums, "grid", split_axis=0, concat_axis=0, tiled=True).reshape(
        devices * capacity, members
    )
    first_row = my_index * block_dev
    my_homes = lax.dynamic_slice_in_dim(pair_home, first_row, block_dev, 0).reshape(entries)
    order_row = lax.broadcasted_iota(jnp.int32, (entries, entries), 0)
    order_col = lax.broadcasted_iota(jnp.int32, (entries, entries), 1)
    earlier = (my_homes[:, None] == my_homes[None, :]) & (order_col < order_row)
    my_position = jnp.sum(earlier.astype(jnp.int32), axis=1)
    item_index = my_homes * capacity + my_position
    pair_sums = received[item_index].reshape(block_dev, pair_count, members)
    innovation = jnp.sum(localization[:, :, None] * pair_sums, axis=1)
    projected = jnp.einsum("bmi,bm->bi", weights, innovation, precision=lax.Precision.HIGHEST)
    mean_weights = jnp.einsum("bji,bi->bj", weights, projected, precision=lax.Precision.HIGHEST) / (
        members - 1
    )
    transform = (weights + mean_weights[:, :, None]).astype(jnp.bfloat16)
    column_totals = jnp.sum(transform.astype(jnp.float32), axis=1)
    inverse = (
        jnp.zeros((blocks_all,), jnp.int32)
        .at[owner_slot]
        .set(jnp.arange(blocks_all, dtype=jnp.int32))
    )
    ordered = ensemble[:, inverse, :]
    owned = lax.all_to_all(ordered, "grid", split_axis=1, concat_axis=0, tiled=True)
    states = owned.reshape(members, LEV, block_dev, points)
    ens_mean = jnp.sum(states, axis=0, dtype=jnp.float32) / members
    product = jnp.einsum("jlbp,bji->ilbp", states, transform, preferred_element_type=jnp.float32)
    analysis = (product + ens_mean[None] * (1.0 - column_totals).T[:, None, :, None]).astype(
        jnp.bfloat16
    )
    returned = lax.all_to_all(
        analysis.reshape(members * LEV, block_dev, points),
        "grid",
        split_axis=0,
        concat_axis=1,
        tiled=True,
    )
    result = returned[:, owner_slot, :]
    return (result, mean_weights)


def per_device(ensemble, owner_slot, weights, *rest):
    rows_here = ensemble.shape[0]
    block_dev = weights.shape[0]
    whole_members = rows_here % LEV == 0
    if whole_members and (rows_here // LEV) * block_dev % 16 == 0:
        return fused(ensemble, owner_slot, weights, *rest)
    return staged(ensemble, owner_slot, weights, *rest)


def solution(mesh):
    placed = (
        P(("groups", "grid"), None, None),
        P("groups"),
        P(("groups", "grid"), None, None),
        P(("groups", "grid"), None, None),
        P(("groups", "grid"), None),
        P(("groups", "grid")),
        P("groups", None),
        P("groups", None),
        P(("groups", "grid"), None),
    )
    return jax.shard_map(
        per_device,
        mesh=mesh,
        in_specs=placed,
        out_specs=(P(("groups", "grid"), None, None), P(("groups", "grid"), None)),
        check_vma=False,
    )
```

```python
import functools

import jax
import jax.numpy as jnp
from jax import lax
from jax.experimental import pallas as pl
from jax.experimental.pallas import tpu as pltpu
from jax.sharding import PartitionSpec as P

LEV = 8
LANES = 128
F32 = jnp.float32
BF16 = jnp.bfloat16
HIGHEST = lax.Precision.HIGHEST


def iota(shape, dim):
    return lax.broadcasted_iota(jnp.int32, shape, dim)


def one_hot(cond):
    return jnp.where(cond, 1.0, 0.0).astype(BF16)


def dot(a, b):
    return jnp.dot(a, b, preferred_element_type=F32)


def dot_nt(a, b, precision=None):
    return lax.dot_general(
        a, b, (((1,), (1,)), ((), ())), preferred_element_type=F32, precision=precision
    )


def peer_order(n):
    return [(n // 4 - 1 + k) % (n - 1) + 1 for k in range(n - 1)]


def fused_kernel(
    dims,
    ens_hbm,
    owner_hbm,
    weights_hbm,
    obs_hbm,
    dep_hbm,
    count_hbm,
    home_hbm,
    index_hbm,
    loc_hbm,
    back_box,
    scatter_hbm,
    mw_hbm,
    ens_ref,
    owner_ref,
    weights_ref,
    obs_ref,
    dep_ref,
    count_ref,
    home_ref,
    index_ref,
    loc_ref,
    mw_ref,
    obs_box,
    send_box,
    recv_box,
    ret_box,
    gather_mat,
    scatter_mat,
    mix_mat,
    gain_ref,
    load_sem,
    ens_sem,
    own_sem,
    obs_send,
    obs_recv,
    fwd_send,
    fwd_recv,
    bwd_send,
    bwd_recv,
):
    n, groups = dims
    me = lax.axis_index("grid")
    rows_here, blocks, points = ens_ref.shape
    block_dev, members, _ = weights_ref.shape
    obs_dev = obs_ref.shape[0]
    pair_count = home_ref.shape[0]
    held = rows_here // LEV
    slab = held * block_dev
    full = n * slab
    lev_group = LEV // groups
    width = lev_group * points
    packed = obs_dev // 2
    peers = peer_order(n)

    barrier = pltpu.get_barrier_semaphore()
    for k in peers:
        pl.semaphore_signal(
            barrier,
            inc=1,
            device_id={"grid": lax.rem(me + k, n)},
            device_id_type=pl.DeviceIdType.MESH,
        )

    def level_rows(g, m):
        return pl.ds(m * LEV + g * lev_group, lev_group)

    def ens_load(g, m):
        rows = level_rows(g, m)
        return pltpu.make_async_copy(ens_hbm.at[rows], ens_ref.at[rows], ens_sem.at[g, m])

    def own_return(g):
        return pltpu.make_async_copy(ret_box.at[g, me], back_box.at[g, me], own_sem.at[g])

    small = (
        (owner_hbm, owner_ref),
        (obs_hbm, obs_ref),
        (dep_hbm, dep_ref),
        (count_hbm, count_ref),
        (home_hbm, home_ref),
        (index_hbm, index_ref),
        (loc_hbm, loc_ref),
        (weights_hbm, weights_ref),
    )
    loads = [
        pltpu.make_async_copy(src, dst, load_sem.at[i]) for i, (src, dst) in enumerate(small)
    ]
    loads[0].start()
    for g in range(groups):
        for m in range(held):
            ens_load(g, m).start()
    for load in loads[1:]:
        load.start()

    r = iota((full, 1), 0)
    row_key = (r // block_dev % held) * blocks + (r // slab) * block_dev + r % block_dev
    loads[0].wait()
    owner = jnp.concatenate([owner_ref[...]] * held, axis=1)
    col_key = owner + iota((1, full), 1) // blocks * blocks
    gather_mat[...] = one_hot(row_key == col_key)

    def arrange(g):
        for m in range(held):
            ens_load(g, m).wait()
        cols = []
        for l in range(g * lev_group, (g + 1) * lev_group):
            cols.append(
                jnp.concatenate([ens_ref[m * LEV + l] for m in range(held)], axis=0)
            )
        state = jnp.concatenate(cols, axis=1)
        sorted_state = dot(gather_mat[...], state).astype(BF16)
        send_box[g] = sorted_state.reshape(n, slab, width)
        recv_box[g, pl.ds(me, 1)] = send_box[g, pl.ds(me, 1)]

    def obs_copy(k):
        to = lax.rem(me + k, n)
        return pltpu.make_async_remote_copy(
            src_ref=obs_box.at[me],
            dst_ref=obs_box.at[me],
            send_sem=obs_send.at[k],
            recv_sem=obs_recv.at[me],
            device_id={"grid": to},
            device_id_type=pl.DeviceIdType.MESH,
        )

    def box_copy(src, dst, send_sem, recv_sem, g, k):
        to = lax.rem(me + k, n)
        return pltpu.make_async_remote_copy(
            src_ref=src.at[g, to],
            dst_ref=dst.at[g, me],
            send_sem=send_sem.at[g, k],
            recv_sem=recv_sem.at[g, me],
            device_id={"grid": to},
            device_id_type=pl.DeviceIdType.MESH,
        )

    def box_arrival(dst, send_sem, recv_sem, g, k):
        src = lax.rem(me + k, n)
        return pltpu.make_async_remote_copy(
            src_ref=dst.at[g, src],
            dst_ref=dst.at[g, src],
            send_sem=send_sem.at[g, k],
            recv_sem=recv_sem.at[g, src],
            device_id={"grid": src},
            device_id_type=pl.DeviceIdType.MESH,
        )

    arrange(0)
    pl.semaphore_wait(barrier, n - 1)
    for k in peers:
        box_copy(send_box, recv_box, fwd_send, fwd_recv, 0, k).start()

    for load in loads[1:]:
        load.wait()
    lane = iota((obs_dev, points), 1)
    dep = dep_ref[...].astype(F32)
    square = iota((obs_dev, obs_dev), 0) == iota((obs_dev, obs_dev), 1)
    count = jnp.sum(jnp.where(square, count_ref[...], 0), axis=1, keepdims=True)
    masked = jnp.where(lane < count, dep, 0.0).astype(BF16)
    cross = dot_nt(masked, obs_ref[...].reshape(obs_dev * members, points))
    row = iota((obs_dev, LANES), 0)
    lane_block = iota((obs_dev, LANES), 1) // members
    per_row = LANES // members
    sums = jnp.zeros((obs_dev, LANES), F32)
    for t in range(obs_dev * members // LANES):
        piece = cross[:, t * LANES : (t + 1) * LANES]
        sums = sums + jnp.where(row == lane_block + t * per_row, piece, 0.0)
    fold = one_hot(iota((packed, obs_dev), 0) == iota((packed, obs_dev), 1) // 2)
    obs_box[pl.ds(me, 1)] = dot(fold, sums.astype(BF16)).astype(BF16)[None]

    for k in peers:
        obs_copy(k).start()
    for g in range(1, groups):
        arrange(g)
        for k in peers:
            box_copy(send_box, recv_box, fwd_send, fwd_recv, g, k).start()

    same = one_hot(iota((full, full), 0) == iota((full, full), 1))
    scatter_mat[...] = dot_nt(same, gather_mat[...]).astype(BF16)
    scatter_store = pltpu.make_async_copy(scatter_mat, scatter_hbm, load_sem.at[len(loads)])
    scatter_store.start()

    for k in peers:
        src = lax.rem(me + k, n)
        pltpu.make_async_remote_copy(
            src_ref=obs_box.at[src],
            dst_ref=obs_box.at[src],
            send_sem=obs_send.at[k],
            recv_sem=obs_recv.at[src],
            device_id={"grid": src},
            device_id_type=pl.DeviceIdType.MESH,
        ).wait_recv()
    all_sums = obs_box[...].reshape(n * packed, LANES).astype(F32)
    mine = one_hot(
        iota((block_dev, blocks), 1) == iota((block_dev, blocks), 0) + me * block_dev
    )
    home = dot_nt(mine, home_ref[...].astype(F32).astype(BF16)).astype(jnp.int32)
    index = dot_nt(mine, index_ref[...].astype(F32).astype(BF16)).astype(jnp.int32)
    spot = home * packed + index // 2
    odd = index % 2
    loc = loc_ref[...]
    col = iota((block_dev, n * packed), 1)
    pick = [jnp.zeros((block_dev, n * packed), F32) for _ in range(2)]
    for k in range(pair_count):
        hit = col == spot[:, k : k + 1]
        for parity in range(2):
            gate = jnp.where(odd[:, k : k + 1] == parity, loc[:, k : k + 1], 0.0)
            pick[parity] = pick[parity] + jnp.where(hit, gate, 0.0)
    even_part = jnp.dot(pick[0], all_sums, precision=HIGHEST, preferred_element_type=F32)
    odd_part = jnp.dot(pick[1], all_sums, precision=HIGHEST, preferred_element_type=F32)
    innovation = even_part[:, :members] + odd_part[:, members:]

    weights = weights_ref[...]
    flat = weights.reshape(block_dev * members, members)
    twice = jnp.concatenate([innovation, innovation], axis=1)
    spread = jnp.concatenate([twice] * (block_dev // 2), axis=1)
    spread_row = iota((block_dev, block_dev * members), 0)
    spread_col = iota((block_dev, block_dev * members), 1) // members
    spread = jnp.where(spread_row == spread_col, spread, 0.0)
    projected = jnp.dot(spread, flat, precision=HIGHEST, preferred_element_type=F32)
    mean_w = jnp.sum(weights * projected[:, None, :], axis=2, keepdims=True) / (members - 1)
    mw_ref[...] = jnp.sum(weights * projected[:, None, :], axis=2) / (members - 1)
    mw_store = pltpu.make_async_copy(mw_ref, mw_hbm, load_sem.at[len(loads) + 1])
    mw_store.start()
    transform = (weights + mean_w).astype(BF16).reshape(block_dev * members, members)

    rr = iota((full, full), 0)
    cc = iota((full, full), 1)
    turn = one_hot((rr // block_dev == cc % members) & (rr % block_dev == cc // members))
    turned = dot(turn, transform).astype(BF16)
    repeat = one_hot(iota((full, members), 0) // block_dev == iota((full, members), 1))
    dense = dot_nt(repeat, turned)
    mix_mat[...] = jnp.where(rr % block_dev == cc % block_dev, dense, 0.0).astype(BF16)
    totals = dot(mix_mat[...], jnp.ones((full, width), BF16))
    gain_ref[...] = (1.0 - totals) * (1.0 / members)
    sum_mat = one_hot(iota((block_dev, full), 0) == iota((block_dev, full), 1) % block_dev)

    for g in range(groups):
        for k in peers:
            box_arrival(recv_box, fwd_send, fwd_recv, g, n - k).wait_recv()
        state = recv_box[g].reshape(full, width)
        product = dot(mix_mat[...], state).reshape(members, block_dev, width)
        member_sum = dot(sum_mat, state)
        gain = gain_ref[...].reshape(members, block_dev, width)
        analysis = (product + gain * member_sum[None]).astype(BF16)
        ret_box[g] = analysis.reshape(n, slab, width)
        own_return(g).start()
        for k in peers:
            box_copy(ret_box, back_box, bwd_send, bwd_recv, g, k).start()

    for k in peers:
        obs_copy(k).wait_send()
        for g in range(groups):
            box_copy(send_box, recv_box, fwd_send, fwd_recv, g, k).wait_send()
            box_copy(ret_box, back_box, bwd_send, bwd_recv, g, k).wait_send()
    scatter_store.wait()
    mw_store.wait()
    for g in range(groups):
        own_return(g).wait()
        for k in peers:
            box_arrival(back_box, bwd_send, bwd_recv, g, n - k).wait_recv()


def restore_kernel(
    back_hbm,
    scatter_hbm,
    mw_hbm,
    out_hbm,
    mw_out,
    back_ref,
    scatter_ref,
    mw_ref,
    out_ref,
    fixed_sem,
    in_sem,
    out_sem,
):
    groups, n, slab, width = back_ref.shape
    held, _, blocks, points = out_ref.shape
    lev_group = width // points
    scatter_load = pltpu.make_async_copy(scatter_hbm, scatter_ref, fixed_sem.at[0])
    mw_load = pltpu.make_async_copy(mw_hbm, mw_ref, fixed_sem.at[1])
    mw_store = pltpu.make_async_copy(mw_ref, mw_out, fixed_sem.at[2])

    def load(g):
        return pltpu.make_async_copy(back_hbm.at[g], back_ref.at[g], in_sem.at[g])

    def store(l):
        return pltpu.make_async_copy(out_ref.at[:, l], out_hbm.at[:, l], out_sem.at[l])

    step = 2 * points
    scatter_load.start()
    for g in range(groups):
        load(g).start()
    mw_load.start()
    scatter_load.wait()
    for g in range(groups):
        load(g).wait()
        for c in range(width // step):
            state = back_ref[g, :, :, c * step : (c + 1) * step].reshape(n * slab, step)
            final = dot(scatter_ref[...], state).astype(BF16)
            for t in range(2):
                l = g * lev_group + c * 2 + t
                for m in range(held):
                    out_ref[m, l] = final[
                        m * blocks : (m + 1) * blocks, t * points : (t + 1) * points
                    ]
                store(l).start()
    mw_load.wait()
    mw_store.start()
    mw_store.wait()
    for l in range(LEV):
        store(l).wait()


def fused(
    ensemble,
    owner_slot,
    weights,
    obs_members,
    departures,
    obs_count,
    pair_home,
    pair_index,
    localization,
    groups=2,
):
    n = lax.axis_size("grid")
    rows_here, blocks, points = ensemble.shape
    block_dev, members, _ = weights.shape
    held = rows_here // LEV
    slab = held * block_dev
    full = n * slab
    width = LEV // groups * points
    obs_dev = obs_members.shape[0]
    box = pltpu.VMEM((groups, n, slab, width), BF16)
    hbm = pl.BlockSpec(memory_space=pltpu.HBM)
    operands = (
        ensemble,
        owner_slot.reshape(1, blocks),
        weights,
        obs_members,
        departures,
        obs_count.reshape(1, obs_dev),
        pair_home.T,
        pair_index.T,
        localization,
    )
    back, scatter, mean_weights = pl.pallas_call(
        functools.partial(fused_kernel, (n, groups)),
        out_shape=(
            jax.ShapeDtypeStruct((groups, n, slab, width), BF16),
            jax.ShapeDtypeStruct((full, full), BF16),
            jax.ShapeDtypeStruct((block_dev, members), F32),
        ),
        in_specs=[hbm] * 9,
        out_specs=(hbm, hbm, hbm),
        scratch_shapes=[
            *[pltpu.VMEM(arg.shape, arg.dtype) for arg in operands],
            pltpu.VMEM((block_dev, members), F32),
            pltpu.VMEM((n, obs_dev // 2, LANES), BF16),
            box,
            box,
            box,
            pltpu.VMEM((full, full), BF16),
            pltpu.VMEM((full, full), BF16),
            pltpu.VMEM((full, full), BF16),
            pltpu.VMEM((full, width), F32),
            pltpu.SemaphoreType.DMA((len(operands) + 1,)),
            pltpu.SemaphoreType.DMA((groups, held)),
            pltpu.SemaphoreType.DMA((groups,)),
            pltpu.SemaphoreType.DMA((n,)),
            pltpu.SemaphoreType.DMA((n,)),
            pltpu.SemaphoreType.DMA((groups, n)),
            pltpu.SemaphoreType.DMA((groups, n)),
            pltpu.SemaphoreType.DMA((groups, n)),
            pltpu.SemaphoreType.DMA((groups, n)),
        ],
        compiler_params=pltpu.CompilerParams(
            collective_id=0, has_side_effects=True, vmem_limit_bytes=60 * 2**20
        ),
    )(*operands)
    analysis, mean_weights = pl.pallas_call(
        restore_kernel,
        out_shape=(
            jax.ShapeDtypeStruct((held, LEV, blocks, points), BF16),
            jax.ShapeDtypeStruct((block_dev, members), F32),
        ),
        in_specs=[hbm] * 3,
        out_specs=(hbm, hbm),
        scratch_shapes=[
            pltpu.VMEM((groups, n, slab, width), BF16),
            pltpu.VMEM((full, full), BF16),
            pltpu.VMEM((block_dev, members), F32),
            pltpu.VMEM((held, LEV, blocks, points), BF16),
            pltpu.SemaphoreType.DMA((3,)),
            pltpu.SemaphoreType.DMA((groups,)),
            pltpu.SemaphoreType.DMA((LEV,)),
        ],
        compiler_params=pltpu.CompilerParams(vmem_limit_bytes=60 * 2**20),
    )(back, scatter, mean_weights)
    return analysis.reshape(ensemble.shape), mean_weights


def staged(
    ensemble,
    owner_slot,
    weights,
    obs_members,
    departures,
    obs_count,
    pair_home,
    pair_index,
    localization,
):
    devices = lax.axis_size("grid")
    my_index = lax.axis_index("grid")
    rows_here, blocks_all, points = ensemble.shape
    block_dev = weights.shape[0]
    members = weights.shape[1]
    pair_count = pair_home.shape[1]
    entries = block_dev * pair_count
    capacity = max(2, 2 * entries // devices)
    slot_pos = lax.broadcasted_iota(jnp.int32, departures.shape, 1)
    masked = jnp.where(slot_pos < obs_count[:, None], departures, jnp.zeros_like(departures))
    homes_all = pair_home.reshape(devices, entries)
    index_all = pair_index.reshape(devices, entries)
    matches = homes_all == my_index
    position = jnp.cumsum(matches.astype(jnp.int32), axis=1) - 1
    slot_ids = jnp.arange(capacity, dtype=jnp.int32)
    select = matches[:, None, :] & (position[:, None, :] == slot_ids[None, :, None])
    picked = jnp.sum(jnp.where(select, index_all[:, None, :], 0), axis=2)
    filled = jnp.any(select, axis=2)
    own_sums = jnp.einsum("okp,op->ok", obs_members, masked, preferred_element_type=jnp.float32)
    send_sums = jnp.where(filled[:, :, None], own_sums[picked], jnp.zeros((), jnp.float32))
    received = lax.all_to_all(send_sums, "grid", split_axis=0, concat_axis=0, tiled=True).reshape(
        devices * capacity, members
    )
    first_row = my_index * block_dev
    my_homes = lax.dynamic_slice_in_dim(pair_home, first_row, block_dev, 0).reshape(entries)
    order_row = lax.broadcasted_iota(jnp.int32, (entries, entries), 0)
    order_col = lax.broadcasted_iota(jnp.int32, (entries, entries), 1)
    earlier = (my_homes[:, None] == my_homes[None, :]) & (order_col < order_row)
    my_position = jnp.sum(earlier.astype(jnp.int32), axis=1)
    item_index = my_homes * capacity + my_position
    pair_sums = received[item_index].reshape(block_dev, pair_count, members)
    innovation = jnp.sum(localization[:, :, None] * pair_sums, axis=1)
    projected = jnp.einsum("bmi,bm->bi", weights, innovation, precision=lax.Precision.HIGHEST)
    mean_weights = jnp.einsum("bji,bi->bj", weights, projected, precision=lax.Precision.HIGHEST) / (
        members - 1
    )
    transform = (weights + mean_weights[:, :, None]).astype(jnp.bfloat16)
    column_totals = jnp.sum(transform.astype(jnp.float32), axis=1)
    inverse = (
        jnp.zeros((blocks_all,), jnp.int32)
        .at[owner_slot]
        .set(jnp.arange(blocks_all, dtype=jnp.int32))
    )
    ordered = ensemble[:, inverse, :]
    owned = lax.all_to_all(ordered, "grid", split_axis=1, concat_axis=0, tiled=True)
    states = owned.reshape(members, LEV, block_dev, points)
    ens_mean = jnp.sum(states, axis=0, dtype=jnp.float32) / members
    product = jnp.einsum("jlbp,bji->ilbp", states, transform, preferred_element_type=jnp.float32)
    analysis = (product + ens_mean[None] * (1.0 - column_totals).T[:, None, :, None]).astype(
        jnp.bfloat16
    )
    returned = lax.all_to_all(
        analysis.reshape(members * LEV, block_dev, points),
        "grid",
        split_axis=0,
        concat_axis=1,
        tiled=True,
    )
    result = returned[:, owner_slot, :]
    return (result, mean_weights)


def per_device(ensemble, owner_slot, weights, *rest):
    rows_here = ensemble.shape[0]
    block_dev = weights.shape[0]
    whole_members = rows_here % LEV == 0
    if whole_members and (rows_here // LEV) * block_dev % 16 == 0:
        return fused(ensemble, owner_slot, weights, *rest)
    return staged(ensemble, owner_slot, weights, *rest)


def solution(mesh):
    placed = (
        P(("groups", "grid"), None, None),
        P("groups"),
        P(("groups", "grid"), None, None),
        P(("groups", "grid"), None, None),
        P(("groups", "grid"), None),
        P(("groups", "grid")),
        P("groups", None),
        P("groups", None),
        P(("groups", "grid"), None),
    )
    return jax.shard_map(
        per_device,
        mesh=mesh,
        in_specs=placed,
        out_specs=(P(("groups", "grid"), None, None), P(("groups", "grid"), None)),
        check_vma=False,
    )
```
